256 devices in a mesh: rows: 16 (over z, core), blk: 16 (over x, y).
Axes of the slice: x: 4, y: 4, z: 8, core: 2. Of those that a mesh axis runs over, the one named last changes fastest.
Arguments:
- jacobian: float32 [65536, 4096], P('rows', 'blk'), may hold values from -6 to 6
- row_weight: float32 [65536], P('rows'), may hold values from 0.3 to 3
- col_scale: float32 [4096], P('blk'), may hold values from 0.3 to 3
- round_count: int32 [2], replicated, may hold values from 12 to 24, as said below
- move_flag: int32 [2, 16], P(None, 'blk'), may hold values 0 or 1
Outputs:
- rotated: float32 [65536, 4096], P('rows', 'blk')
- orth_basis: float32 [4096, 4096], P('rows', 'blk')
The draws below stay inside these ranges and needn't reach their ends.
Inputs may be any that keep to these rules, and one draw needn't show every extreme that they name: `round_count`: one entry equals 24.
All inputs are finite; a program needn't handle non-finite values. No bound on the sum of `move_flag` on one device may be relied on, other than what follows from the above.
Results may differ from the reference program's by a relative error of at most 0.0004.
Values sent between devices are 32-bit elements; how exact they have to be, the bound alone decides.
A program may use at most 64 MiB of HBM per device.

```python
import math
import jax
import jax.numpy as jnp
from jax import lax

BLOCK = 128
STEPS = 2
ROUNDS = 24
ROWS = 65536
COLS = 4096
N_BLK = 16


def draw_round_count(key, part):
    key = jax.random.fold_in(key, 7)
    count_key, place_key = jax.random.split(key)
    counts = jax.random.randint(count_key, (STEPS,), ROUNDS // 2, ROUNDS)
    where_top = jax.random.randint(place_key, (), 0, STEPS)
    return jnp.where(jnp.arange(STEPS) == where_top, ROUNDS, counts).astype(jnp.int32)


def place_ends(entries, own_key, smallest, high):
    extent = entries.shape
    spot = [jax.random.randint(jax.random.fold_in(own_key, axis), (), 0, extent[axis]) for axis in range(len(extent))]
    entries = entries.at[tuple(spot)].set(smallest)
    longest = extent.index(max(extent))
    spot[longest] = (spot[longest] + 1) % extent[longest]
    return entries.at[tuple(spot)].set(high)


def levels(rng, dims, shards, least, high):
    loudness = 1.0
    for position, shards_of in shards:
        draws = jax.random.uniform(jax.random.fold_in(jax.random.fold_in(rng, 6), position), (shards_of,), jnp.float32, least / len(shards), high / len(shards))
        loudness = loudness * jnp.repeat(jnp.exp(draws), dims[position] // shards_of).reshape((-1,) + (1,) * (len(dims) - 1 - position))
    return loudness


def bell_draw(own_key, dims, spread, bound, pieces=(), kind=jnp.bfloat16):
    level = levels(own_key, dims, pieces, -0.22, 0.18) if pieces else 1.0
    entries = jax.random.normal(own_key, dims, jnp.float32) * spread * level
    return jnp.minimum(jnp.maximum(entries, -bound), bound).astype(kind)


def setup_inputs(seed: int = 0) -> dict:
    key_of = jax.random.split(jax.random.key(seed), 6)
    return {
        "jacobian": bell_draw(key_of[0], (ROWS, COLS), 1.0, 6.0, ((0, 16), (1, 16)), jnp.float32),
        "row_weight": jnp.clip(jnp.exp(math.log(3.0) - 2.3025851 * jax.random.uniform(key_of[1], (ROWS,), jnp.float32) ** levels(key_of[1], (ROWS,), ((0, 16),), -0.2, 0.2)), 0.3, 3.0),
        "col_scale": jnp.clip(jnp.exp(math.log(3.0) - 2.3025851 * jax.random.uniform(key_of[2], (COLS,), jnp.float32) ** levels(key_of[2], (COLS,), ((0, 16),), -0.2, 0.2)), 0.3, 3.0),
        "round_count": draw_round_count(jax.random.fold_in(key_of[5], 71), 0),
        "move_flag": place_ends((jax.random.randint(key_of[4], (STEPS, N_BLK), 0, 2) < 1).astype(jnp.int32), jax.random.fold_in(key_of[4], 1), 0, 1),
    }


def rotate_pairs(matrix, cosine, sine_val, axis_pos):
    half_size = cosine.shape[0]
    if axis_pos == 0:
        upper = matrix[:half_size]
        lower = matrix[half_size:]
        cos_b = cosine[:, None]
        sin_b = sine_val[:, None]
    else:
        upper = matrix[:, :half_size]
        lower = matrix[:, half_size:]
        cos_b = cosine[None, :]
        sin_b = sine_val[None, :]
    return jnp.concatenate([cos_b * upper - sin_b * lower, sin_b * upper + cos_b * lower], axis_pos)

def cycle_lower(matrix, axis_pos, half_size):
    if axis_pos == 0:
        return jnp.concatenate([matrix[:half_size], jnp.roll(matrix[half_size:], -1, 0)], 0)
    return jnp.concatenate([matrix[:, :half_size], jnp.roll(matrix[:, half_size:], -1, 1)], 1)

def inner_rounds(pair_matrix, count):
    half_size = pair_matrix.shape[0] // 2
    transform = jnp.eye(2 * half_size, dtype=jnp.float32)

    def one_round(index, state_pair):
        gram_now, trans_now = state_pair
        diag_vals = jnp.diagonal(gram_now)
        first_diag = diag_vals[:half_size]
        second_diag = diag_vals[half_size:]
        cross_vals = jnp.diagonal(gram_now[:half_size, half_size:])
        diff_vals = second_diag - first_diag
        radius = jnp.sqrt(diff_vals * diff_vals + 4.0 * cross_vals * cross_vals)
        signs = jnp.where(diff_vals >= 0.0, 1.0, -1.0).astype(jnp.float32)
        tangent = signs * 2.0 * cross_vals / (jnp.abs(diff_vals) + radius)
        cosine = 1.0 / jnp.sqrt(1.0 + tangent * tangent)
        sine_val = cosine * tangent
        gram_now = rotate_pairs(gram_now, cosine, sine_val, 0)
        gram_now = rotate_pairs(gram_now, cosine, sine_val, 1)
        trans_now = rotate_pairs(trans_now, cosine, sine_val, 1)
        gram_now = cycle_lower(cycle_lower(gram_now, 0, half_size), 1, half_size)
        trans_now = cycle_lower(trans_now, 1, half_size)
        return (gram_now, trans_now)
    return lax.fori_loop(0, count, one_round, (pair_matrix, transform))

def reference(jacobian, row_weight, col_scale, round_count, move_flag):
    scaled = jacobian * row_weight[:, None] * col_scale[None, :]
    pairs = scaled.reshape(ROWS, N_BLK, 2 * BLOCK).transpose(1, 0, 2)
    basis_cols = jnp.eye(COLS, dtype=jnp.float32).reshape(COLS, N_BLK, 2 * BLOCK).transpose(1, 0, 2)
    for step_index in range(STEPS):
        count = round_count[step_index]

        def solve(pair_item):
            block_x, block_w = pair_item
            pair_matrix = lax.dot_general(block_x, block_x, (((0,), (0,)), ((), ())), precision=lax.Precision.HIGHEST, preferred_element_type=jnp.float32)
            unused, transform = inner_rounds(pair_matrix, count)
            new_x = jnp.dot(block_x, transform, precision=lax.Precision.HIGHEST, preferred_element_type=jnp.float32)
            new_w = jnp.dot(block_w, transform, precision=lax.Precision.HIGHEST, preferred_element_type=jnp.float32)
            return (new_x, new_w)
        pairs, basis_cols = lax.map(solve, (pairs, basis_cols))
        moves_left = (move_flag[step_index] == 1)[:, None, None]
        travel_x = jnp.where(moves_left, pairs[:, :, :BLOCK], pairs[:, :, BLOCK:])
        stay_x = jnp.where(moves_left, pairs[:, :, BLOCK:], pairs[:, :, :BLOCK])
        travel_w = jnp.where(moves_left, basis_cols[:, :, :BLOCK], basis_cols[:, :, BLOCK:])
        stay_w = jnp.where(moves_left, basis_cols[:, :, BLOCK:], basis_cols[:, :, :BLOCK])
        pairs = jnp.concatenate([stay_x, jnp.roll(travel_x, 1, 0)], 2)
        basis_cols = jnp.concatenate([stay_w, jnp.roll(travel_w, 1, 0)], 2)
    rotated = pairs.transpose(1, 0, 2).reshape(ROWS, COLS)
    orth_basis = basis_cols.transpose(1, 0, 2).reshape(COLS, COLS)
    return (rotated, orth_basis)
```

```python
import jax
import jax.numpy as jnp
from jax import lax
from jax.experimental import pallas as pl
from jax.experimental.pallas import tpu as pltpu
from jax.sharding import PartitionSpec as P

MESH = pl.DeviceIdType.MESH
B = 128
ROUNDS = 24
CH = 256
F32 = jnp.float32
BF16 = jnp.bfloat16


def split(x):
    high = x.astype(BF16)
    return high, (x - high.astype(F32)).astype(BF16)


def rotation(first, second, cross, live):
    diff = second - first
    radius = jnp.sqrt(diff * diff + 4.0 * cross * cross)
    signs = jnp.where(diff >= 0.0, 1.0, -1.0)
    tangent = signs * 2.0 * cross / (jnp.abs(diff) + radius)
    cosine = 1.0 / jnp.sqrt(1.0 + tangent * tangent)
    sine = cosine * tangent
    return jnp.where(live, cosine, 1.0), jnp.where(live, sine, 0.0)


def tile(k):
    return pl.ds(8 * k, 8)


def spaced(k, start=0):
    return pl.ds(start + k, 8, stride=16)


def inner_rounds(count, gram, q, a, c, e, d, ccol, scol):
    count = jnp.full((8, B), count, jnp.int32)
    lane = lax.broadcasted_iota(jnp.int32, (8, B), 1)
    sub = lax.broadcasted_iota(jnp.int32, (8, B), 0)
    low = lane % 16
    on_diag = (lane // 16) == sub
    nxt = (lane + (B - 1)) % B
    nlow = nxt % 16
    on_next = (nxt // 16) == sub
    ccol[...] = jnp.transpose(gram[B : 2 * B, :])
    for k in range(16):
        a[tile(k), :] = gram[spaced(k), :]
        c[tile(k), :] = gram[spaced(k, B), :]
        e[tile(k), :] = ccol[spaced(k), :]
        d[tile(k), :] = gram[spaced(k, 2 * B), :]
    rows = lax.broadcasted_iota(jnp.int32, (2 * B, 2 * B), 0)
    cols = lax.broadcasted_iota(jnp.int32, (2 * B, 2 * B), 1)
    q[...] = (rows == cols).astype(F32)

    def pick(ref):
        acc = jnp.zeros((8, B), F32)
        for k in range(16):
            acc = jnp.where(low == k, ref[tile(k), :], acc)
        return total(jnp.where(on_diag, acc, 0.0))

    def total(x):
        return jnp.broadcast_to(jnp.sum(x, axis=0, keepdims=True), (8, B))

    def spread(cs, sn):
        ccol[...] = jnp.transpose(jnp.broadcast_to(cs[0:1], (B, B)))
        scol[...] = jnp.transpose(jnp.broadcast_to(sn[0:1], (B, B)))

    cs, sn = rotation(pick(a), pick(d), pick(c), 0 < count)
    spread(cs, sn)

    def one(index, carry):
        cs, sn = carry
        acc_a = acc_c = acc_d = jnp.zeros((8, B), F32)
        first = None
        for k in range(16):
            before = tile((k - 1) % 16)
            ck, sk = ccol[spaced(k), :], scol[spaced(k), :]
            ak, bk, ek, dk = a[tile(k), :], c[tile(k), :], e[tile(k), :], d[tile(k), :]
            a1 = ck * ak - sk * ek
            e1 = sk * ak + ck * ek
            b1 = ck * bk - sk * dk
            d1 = sk * bk + ck * dk
            a2 = a1 * cs - b1 * sn
            b2 = a1 * sn + b1 * cs
            e2 = e1 * cs - d1 * sn
            d2 = e1 * sn + d1 * cs
            acc_a = jnp.where(low == k, a2, acc_a)
            acc_d = jnp.where(low == k, d2, acc_d)
            acc_c = jnp.where(nlow == k, b2, acc_c)
            a[tile(k), :] = a2
            c[tile(k), :] = pltpu.roll(b2, B - 1, 1)
            d3 = pltpu.roll(d2, B - 1, 1)
            if k == 0:
                first = (e2, d3)
            else:
                e[before, :] = e2
                d[before, :] = d3
        e[tile(15), :] = pltpu.roll(first[0], 7, 0)
        d[tile(15), :] = pltpu.roll(first[1], 7, 0)
        diag_a = total(jnp.where(on_diag, acc_a, 0.0))
        diag_d = pltpu.roll(total(jnp.where(on_diag, acc_d, 0.0)), B - 1, 1)
        diag_c = pltpu.roll(total(jnp.where(on_next, acc_c, 0.0)), B - 1, 1)
        new = rotation(diag_a, diag_d, diag_c, index + 1 < count)
        for k in range(32):
            qa, qb = q[tile(k), 0:B], q[tile(k), B : 2 * B]
            q[tile(k), 0:B] = qa * cs - qb * sn
            q[tile(k), B : 2 * B] = pltpu.roll(qa * sn + qb * cs, B - 1, 1)
        spread(*new)
        return new

    lax.fori_loop(0, ROUNDS, one, (cs, sn))
    extra = ROUNDS - count
    for k in range(32):
        qb = q[tile(k), B : 2 * B]
        for bit in range(5):
            qb = jnp.where((extra >> bit) % 2 == 1, pltpu.roll(qb, 1 << bit, 1), qb)
        q[tile(k), B : 2 * B] = qb


def body(
    counts, flags, x_hbm, out_hbm, w_out,
    x, s, t, tin, u, g, hh, hl, q, qhi, qlo, ra, rc, re, rd, ccol, scol, half, piece, full, w1, w1in, w2, w2in,
    load_sem, store_sem, t_send, t_recv, u_send, u_recv, core_send, core_recv, z_send, z_recv, w_send, w_recv,
):
    row, blk = lax.axis_index("rows"), lax.axis_index("blk")
    n_blk = lax.axis_size("blk")
    z, core = row // 2, row % 2
    chunks = x.shape[0] // CH
    fwd = (row, (blk + 1) % n_blk)
    bwd = (row, (blk + n_blk - 1) % n_blk)
    twin = (row + 1 - 2 * core, blk)
    peers = [(((z + i) % 8) * 2 + core, blk) for i in range(1, 8)]
    owner = row == blk
    next_owner = row == (blk + n_blk - 1) % n_blk
    third_owner = row == (blk + n_blk - 2) % n_blk

    def at(c):
        return pl.ds(pl.multiple_of(c * CH, CH), CH)

    def load(c):
        return pltpu.make_async_copy(x_hbm.at[at(c), :], x.at[at(c), :], load_sem.at[c])

    lax.fori_loop(0, chunks, lambda c, _: (load(c).start(), 0)[1], 0)

    barrier = pltpu.get_barrier_semaphore()
    for device in [bwd, twin] + peers:
        pl.semaphore_signal(barrier, inc=1, device_id=device, device_id_type=MESH)
    pl.semaphore_wait(barrier, 9)

    def remote(src, dst, send, recv, device):
        return pltpu.make_async_remote_copy(
            src_ref=src, dst_ref=dst, send_sem=send, recv_sem=recv, device_id=device, device_id_type=MESH
        )

    def add_gram(block, first):
        high, low = split(block)
        dims = (((0,), (0,)), ((), ()))
        both = lax.dot_general(high, jnp.concatenate([high, low], 1), dims, preferred_element_type=F32)
        small = low.astype(F32)
        small = jnp.sum((small * small).reshape(CH // 8, 8, 2 * B), axis=0)
        hh[...] = hh[...] + both[:, : 2 * B]
        hl[...] = hl[...] + both[:, 2 * B :]
        return small

    def gram(get):
        hh[...] = jnp.zeros_like(hh)
        hl[...] = jnp.zeros_like(hl)
        small = lax.fori_loop(
            0, chunks, lambda c, acc: acc + add_gram(get(c), c), jnp.zeros((8, 2 * B), F32)
        )
        small = jnp.sum(small, axis=0, keepdims=True)
        rows = lax.broadcasted_iota(jnp.int32, (B, B), 0)
        cols = lax.broadcasted_iota(jnp.int32, (B, B), 1)
        for place, (i, j) in enumerate(((0, 0), (0, 1), (1, 1))):
            here, there = pl.ds(i * B, B), pl.ds(j * B, B)
            block = hh[here, there] + (hl[here, there] + jnp.transpose(hl[there, here]))
            if i == j:
                block = block + jnp.where(rows == cols, small[:, i * B : (i + 1) * B], 0.0)
            g[pl.ds(place * B, B), :] = block

    def reduce_all(step):
        mine = pl.ds(pl.multiple_of(core * 192, 8), 192)
        other = pl.ds(pl.multiple_of((1 - core) * 192, 8), 192)
        copy = remote(g.at[other, :], half.at[:, :], core_send.at[2 * step], core_recv.at[2 * step], twin)
        copy.start()
        copy.wait()
        g[mine, :] = g[mine, :] + half[...]
        copies = []
        for i, peer in enumerate(peers):
            rows = pl.ds(pl.multiple_of(core * 192 + (peer[0] // 2) * 24, 8), 24)
            copies.append(remote(
                g.at[rows, :], piece.at[step, i], z_send.at[step, i], z_recv.at[step, i], peer
            ))
            copies[-1].start()
        for copy in copies:
            copy.wait()
        own = pl.ds(pl.multiple_of(core * 192 + z * 24, 8), 24)
        total = g[own, :]
        for i in range(7):
            total = total + piece[step, i]
        done = full.at[step]
        done[own, :] = total
        copies = []
        for i, peer in enumerate(peers):
            copies.append(remote(
                done.at[own, :], done.at[own, :], z_send.at[step, 7 + i], z_recv.at[step, 7 + i], peer
            ))
            copies[-1].start()
        for copy in copies:
            copy.wait()
        copy = remote(done.at[mine, :], done.at[mine, :], core_send.at[2 * step + 1], core_recv.at[2 * step + 1], twin)
        copy.start()
        copy.wait()

    def solve(step):
        reduce_all(step)
        inner_rounds(counts[step], full.at[step], q, ra, rc, re, rd, ccol, scol)
        left = jnp.full((8, B), flags[step, 0], jnp.int32) == 1
        for k in range(32):
            qa, qb = q[tile(k), 0:B], q[tile(k), B : 2 * B]
            q[tile(k), 0:B] = jnp.where(left, qb, qa)
            q[tile(k), B : 2 * B] = jnp.where(left, qa, qb)
        qhi[...], qlo[...] = split(q[...])

    def multiply(block):
        high, low = split(block)
        qh = qhi[...]
        out = jnp.dot(low, qh, preferred_element_type=F32)
        out = out + jnp.dot(high, qlo[...], preferred_element_type=F32)
        return out + jnp.dot(high, qh, preferred_element_type=F32)

    def t_copy(c):
        return remote(t.at[at(c), :], tin.at[at(c), :], t_send.at[c], t_recv.at[c], fwd)

    def u_copy(c):
        return remote(u.at[at(c), :], out_hbm.at[at(c), B : 2 * B], u_send.at[c], u_recv.at[c], fwd)

    def w_copy(step):
        if step == 0:
            return remote(w1.at[:, B : 2 * B], w1in, w_send.at[0], w_recv.at[0], fwd)
        return remote(w2.at[:, B : 2 * B], w2in, w_send.at[1], w_recv.at[1], fwd)

    def loaded(c):
        load(c).wait()
        return x[at(c), :]

    gram(loaded)
    solve(0)

    def first_step(c, _):
        y = multiply(x[at(c), :])
        s[at(c), :] = y[:, :B]
        t[at(c), :] = y[:, B:]
        t_copy(c).start()
        return 0

    lax.fori_loop(0, chunks, first_step, 0)
    @pl.when(owner)
    def _():
        w1[...] = q[...]
        w_copy(0).start()

    @pl.when(jnp.logical_not(owner))
    def _():
        w1[...] = jnp.zeros_like(w1)

    @pl.when(jnp.logical_not(next_owner))
    def _():
        w1in[...] = jnp.zeros_like(w1in)

    def pair(c):
        return jnp.concatenate([s[at(c), :], tin[at(c), :]], 1)

    def arrived(c):
        t_copy(c).wait_recv()
        return pair(c)

    gram(arrived)
    solve(1)

    def stay_copy(c):
        return pltpu.make_async_copy(s.at[at(c), :], out_hbm.at[at(c), 0:B], store_sem.at[c])

    def second_step(c, _):
        y = multiply(pair(c))
        u[at(c), :] = y[:, B:]
        u_copy(c).start()
        s[at(c), :] = y[:, :B]
        stay_copy(c).start()
        return 0

    lax.fori_loop(0, chunks, second_step, 0)

    @pl.when(next_owner)
    def _():
        w_copy(0).wait_recv()

    w2[...] = multiply(jnp.concatenate([w1[:, :B], w1in[...]], 1))
    w_out[:, :B] = w2[:, :B]

    @pl.when(jnp.logical_or(owner, next_owner))
    def _():
        w_copy(1).start()

    @pl.when(jnp.logical_not(jnp.logical_or(next_owner, third_owner)))
    def _():
        w_out[:, B:] = jnp.zeros((2 * B, B), F32)

    def finish(c, _):
        t_copy(c).wait_send()
        u_copy(c).wait_send()
        u_copy(c).wait_recv()
        stay_copy(c).wait()
        return 0

    lax.fori_loop(0, chunks, finish, 0)

    @pl.when(owner)
    def _():
        w_copy(0).wait_send()

    @pl.when(jnp.logical_or(owner, next_owner))
    def _():
        w_copy(1).wait_send()

    @pl.when(jnp.logical_or(next_owner, third_owner))
    def _():
        w_copy(1).wait_recv()
        w_out[:, B:] = w2in[...]


def per_device(jacobian, row_weight, col_scale, round_count, move_flag):
    scaled = jacobian * row_weight[:, None] * col_scale[None, :]
    rows = scaled.shape[0]
    chunks = rows // CH
    anywhere = pl.BlockSpec(memory_space=pl.ANY)
    vmem = pl.BlockSpec(memory_space=pltpu.VMEM)
    smem = pl.BlockSpec(memory_space=pltpu.SMEM)
    dma = pltpu.SemaphoreType.DMA
    square = pltpu.VMEM((B, B), F32)
    wide = pltpu.VMEM((2 * B, 2 * B), F32)
    tall = pltpu.VMEM((2 * B, B), F32)
    column = pltpu.VMEM((rows, B), F32)
    return pl.pallas_call(
        body,
        out_shape=(
            jax.ShapeDtypeStruct((rows, 2 * B), F32),
            jax.ShapeDtypeStruct((2 * B, 2 * B), F32),
        ),
        in_specs=[smem, smem, anywhere],
        out_specs=(anywhere, vmem),
        scratch_shapes=[
            pltpu.VMEM((rows, 2 * B), F32), column, column, column, column,
            pltpu.VMEM((3 * B, B), F32), wide, wide, wide,
            pltpu.VMEM((2 * B, 2 * B), BF16), pltpu.VMEM((2 * B, 2 * B), BF16),
            square, square, square, square, square, square,
            pltpu.VMEM((192, B), F32), pltpu.VMEM((2, 7, 24, B), F32), pltpu.VMEM((2, 3 * B, B), F32),
            wide, tall, wide, tall,
            dma((chunks,)), dma((chunks,)), dma((chunks,)), dma((chunks,)), dma((chunks,)), dma((chunks,)),
            dma((4,)), dma((4,)), dma((2, 14)), dma((2, 14)), dma((2,)), dma((2,)),
        ],
        compiler_params=pltpu.CompilerParams(
            collective_id=0, has_side_effects=True, vmem_limit_bytes=56 * 2**20
        ),
        name="jacobi",
    )(round_count, move_flag, scaled)


def solution(mesh):
    in_specs = (P("rows", "blk"), P("rows"), P("blk"), P(), P(None, "blk"))
    out_specs = (P("rows", "blk"), P("rows", "blk"))
    return jax.shard_map(
        per_device, mesh=mesh, in_specs=in_specs, out_specs=out_specs, check_vma=False
    )
```

```python
import jax
import jax.numpy as jnp
from jax import lax
from jax.experimental import pallas as pl
from jax.experimental.pallas import tpu as pltpu
from jax.sharding import PartitionSpec as P

MESH = pl.DeviceIdType.MESH
B = 128
ROUNDS = 24
CH = 256
F32 = jnp.float32
BF16 = jnp.bfloat16


def split(x):
    high = x.astype(BF16)
    return high, (x - high.astype(F32)).astype(BF16)


def split_rest(x):
    high = x.astype(BF16)
    return high, x - high.astype(F32)


def rotation(first, second, cross, live):
    diff = second - first
    radius = jnp.sqrt(diff * diff + 4.0 * cross * cross)
    signs = jnp.where(diff >= 0.0, 1.0, -1.0)
    tangent = signs * 2.0 * cross / (jnp.abs(diff) + radius)
    cosine = 1.0 / jnp.sqrt(1.0 + tangent * tangent)
    sine = cosine * tangent
    return jnp.where(live, cosine, 1.0), jnp.where(live, sine, 0.0)


def tile(k):
    return pl.ds(8 * k, 8)


def spaced(k, start=0):
    return pl.ds(start + k, 8, stride=16)


def inner_rounds(count, cross, q, a, c, e, d, ccol, scol):
    count = jnp.full((8, B), count, jnp.int32)
    lane = lax.broadcasted_iota(jnp.int32, (8, B), 1)
    sub = lax.broadcasted_iota(jnp.int32, (8, B), 0)
    low = lane % 16
    on_diag = (lane // 16) == sub
    nxt = (lane + (B - 1)) % B
    nlow = nxt % 16
    on_next = (nxt // 16) == sub
    ccol[...] = jnp.transpose(cross[...])
    for k in range(16):
        c[tile(k), :] = cross[spaced(k), :]
        e[tile(k), :] = ccol[spaced(k), :]
    rows = lax.broadcasted_iota(jnp.int32, (2 * B, 2 * B), 0)
    cols = lax.broadcasted_iota(jnp.int32, (2 * B, 2 * B), 1)
    q[...] = (rows == cols).astype(F32)

    def pick(ref):
        acc = jnp.zeros((8, B), F32)
        for k in range(16):
            acc = jnp.where(low == k, ref[tile(k), :], acc)
        return total(jnp.where(on_diag, acc, 0.0))

    def total(x):
        return jnp.broadcast_to(jnp.sum(x, axis=0, keepdims=True), (8, B))

    def spread(cs, sn):
        ccol[...] = jnp.transpose(jnp.broadcast_to(cs[0:1], (B, B)))
        scol[...] = jnp.transpose(jnp.broadcast_to(sn[0:1], (B, B)))

    cs, sn = rotation(pick(a), pick(d), pick(c), 0 < count)
    spread(cs, sn)

    def one(index, carry):
        cs, sn = carry
        acc_a = acc_c = acc_d = jnp.zeros((8, B), F32)
        first = None
        for k in range(16):
            before = tile((k - 1) % 16)
            ck, sk = ccol[spaced(k), :], scol[spaced(k), :]
            ak, bk, ek, dk = a[tile(k), :], c[tile(k), :], e[tile(k), :], d[tile(k), :]
            a1 = ck * ak - sk * ek
            e1 = sk * ak + ck * ek
            b1 = ck * bk - sk * dk
            d1 = sk * bk + ck * dk
            a2 = a1 * cs - b1 * sn
            b2 = a1 * sn + b1 * cs
            e2 = e1 * cs - d1 * sn
            d2 = e1 * sn + d1 * cs
            acc_a = jnp.where(low == k, a2, acc_a)
            acc_d = jnp.where(low == k, d2, acc_d)
            acc_c = jnp.where(nlow == k, b2, acc_c)
            a[tile(k), :] = a2
            c[tile(k), :] = pltpu.roll(b2, B - 1, 1)
            d3 = pltpu.roll(d2, B - 1, 1)
            if k == 0:
                first = (e2, d3)
            else:
                e[before, :] = e2
                d[before, :] = d3
        e[tile(15), :] = pltpu.roll(first[0], 7, 0)
        d[tile(15), :] = pltpu.roll(first[1], 7, 0)
        diag_a = total(jnp.where(on_diag, acc_a, 0.0))
        diag_d = pltpu.roll(total(jnp.where(on_diag, acc_d, 0.0)), B - 1, 1)
        diag_c = pltpu.roll(total(jnp.where(on_next, acc_c, 0.0)), B - 1, 1)
        new = rotation(diag_a, diag_d, diag_c, index + 1 < count)
        for k in range(32):
            qa, qb = q[tile(k), 0:B], q[tile(k), B : 2 * B]
            q[tile(k), 0:B] = qa * cs - qb * sn
            q[tile(k), B : 2 * B] = pltpu.roll(qa * sn + qb * cs, B - 1, 1)
        spread(*new)
        return new

    lax.fori_loop(0, ROUNDS, one, (cs, sn))
    extra = ROUNDS - count
    surplus = [(extra >> bit) % 2 == 1 for bit in range(5)]
    for k in range(32):
        qb = q[tile(k), B : 2 * B]
        for bit in range(5):
            qb = jnp.where(surplus[bit], pltpu.roll(qb, 1 << bit, 1), qb)
        q[tile(k), B : 2 * B] = qb
    return surplus


def undo_moves(d, surplus):
    tiles = [d[tile(k), :] for k in range(16)]
    for bit in range(5):
        move = 1 << bit
        moved = []
        for k in range(16):
            value = pltpu.roll(tiles[(k - move) % 16], move, 1)
            moved.append(value if k >= move else pltpu.roll(value, 1, 0))
        tiles = [jnp.where(surplus[bit], new, old) for new, old in zip(moved, tiles)]
    return tiles


def body(
    counts, flags, x_hbm, out_hbm, w_out,
    x, s, t, tin, sin, u, v, g, hh, hl, q, qhi, qmid, qlo, ra, rc, re, rd, ccol, scol,
    half, piece, full, cross, cross_half, own_piece, far_piece, cross_full, d_out, d_in, w1, w1in, w2, w2in,
    load_sem, store_sem, t_send, t_recv, s_send, s_recv, u_send, u_recv,
    core_send, core_recv, z_send, z_recv, far_send, far_recv, w_send, w_recv, d_send, d_recv,
):
    row, blk = lax.axis_index("rows"), lax.axis_index("blk")
    n_blk = lax.axis_size("blk")
    z, core = row // 2, row % 2
    chunks = x.shape[0] // CH
    mid = chunks // 2
    next_blk = (blk + 1) % n_blk
    last_blk = (blk + n_blk - 1) % n_blk
    fwd, bwd = (row, next_blk), (row, last_blk)
    twin = (row + 1 - 2 * core, blk)
    peers = [(((z + i) % 8) * 2 + core, blk) for i in range(1, 8)]
    far = [(((z + i) % 8) * 2 + core, next_blk) for i in range(8)]
    far_from = [(((z + i) % 8) * 2 + core, last_blk) for i in range(8)]
    owner = row == blk
    next_owner = row == last_blk
    third_owner = row == (blk + n_blk - 2) % n_blk

    def at(c):
        return pl.ds(pl.multiple_of(c * CH, CH), CH)

    def load(c):
        return pltpu.make_async_copy(x_hbm.at[at(c), :], x.at[at(c), :], load_sem.at[c])

    lax.fori_loop(0, chunks, lambda c, _: (load(c).start(), 0)[1], 0)

    barrier = pltpu.get_barrier_semaphore()
    for device in [twin, fwd] + peers + far_from:
        pl.semaphore_signal(barrier, inc=1, device_id=device, device_id_type=MESH)

    def remote(src, dst, send, recv, device):
        return pltpu.make_async_remote_copy(
            src_ref=src, dst_ref=dst, send_sem=send, recv_sem=recv, device_id=device, device_id_type=MESH
        )

    dims = (((0,), (0,)), ((), ()))

    def gram():
        hh[...] = jnp.zeros_like(hh)
        hl[...] = jnp.zeros_like(hl)

        def add(c, acc):
            load(c).wait()
            high, low = split(x[at(c), :])
            both = lax.dot_general(high, jnp.concatenate([high, low], 1), dims, preferred_element_type=F32)
            small = low.astype(F32)
            hh[...] = hh[...] + both[:, : 2 * B]
            hl[...] = hl[...] + both[:, 2 * B :]
            return acc + jnp.sum((small * small).reshape(CH // 8, 8, 2 * B), axis=0)

        small = lax.fori_loop(0, chunks, add, jnp.zeros((8, 2 * B), F32))
        small = jnp.sum(small, axis=0, keepdims=True)
        rows = lax.broadcasted_iota(jnp.int32, (B, B), 0)
        cols = lax.broadcasted_iota(jnp.int32, (B, B), 1)
        for place, (i, j) in enumerate(((0, 0), (0, 1), (1, 1))):
            here, there = pl.ds(i * B, B), pl.ds(j * B, B)
            block = hh[here, there] + (hl[here, there] + jnp.transpose(hl[there, here]))
            if i == j:
                block = block + jnp.where(rows == cols, small[:, i * B : (i + 1) * B], 0.0)
            g[pl.ds(place * B, B), :] = block

    def exchange(index, src, dst):
        copy = remote(src, dst, core_send.at[index], core_recv.at[index], twin)
        copy.start()
        copy.wait()

    def share(step, ref, own):
        copies = []
        for i, peer in enumerate(peers):
            copies.append(remote(
                ref.at[own, :], ref.at[own, :], z_send.at[step, 7 + i], z_recv.at[step, 7 + i], peer
            ))
            copies[-1].start()
        for copy in copies:
            copy.wait()

    def reduce_all():
        mine = pl.ds(pl.multiple_of(core * 192, 8), 192)
        other = pl.ds(pl.multiple_of((1 - core) * 192, 8), 192)
        own = pl.ds(pl.multiple_of(core * 192 + z * 24, 8), 24)
        exchange(0, g.at[other, :], half.at[:, :])
        g[mine, :] = g[mine, :] + half[...]
        copies = []
        for i, peer in enumerate(peers):
            rows = pl.ds(pl.multiple_of(core * 192 + (peer[0] // 2) * 24, 8), 24)
            copies.append(remote(g.at[rows, :], piece.at[i], z_send.at[0, i], z_recv.at[0, i], peer))
            copies[-1].start()
        for copy in copies:
            copy.wait()
        total = g[own, :]
        for i in range(7):
            total = total + piece[i]
        full[own, :] = total
        share(0, full, own)
        exchange(1, full.at[mine, :], full.at[mine, :])

    def reduce_cross(started):
        mine = pl.ds(pl.multiple_of(core * 64, 8), 64)
        other = pl.ds(pl.multiple_of((1 - core) * 64, 8), 64)
        own = pl.ds(pl.multiple_of(core * 64 + z * 8, 8), 8)
        exchange(2, cross.at[:, other, :], cross_half)
        cross[:, mine, :] = cross[:, mine, :] + cross_half[...]
        copies = []
        for i, device in enumerate(far):
            rows = pl.ds(pl.multiple_of(core * 64 + (device[0] // 2) * 8, 8), 8)
            copies.append(remote(cross.at[1, rows, :], far_piece.at[i], far_send.at[i], far_recv.at[i], device))
            copies[-1].start()
        for i, peer in enumerate(peers):
            rows = pl.ds(pl.multiple_of(core * 64 + (peer[0] // 2) * 8, 8), 8)
            copies.append(remote(cross.at[0, rows, :], own_piece.at[i], z_send.at[1, i], z_recv.at[1, i], peer))
            copies[-1].start()
        started()
        for copy in copies:
            copy.wait()
        total = cross[0, own, :] + far_piece[0]
        for i in range(7):
            total = total + (own_piece[i] + far_piece[i + 1])
        cross_full[own, :] = total
        share(1, cross_full, own)
        exchange(3, cross_full.at[mine, :], cross_full.at[mine, :])

    def arrange(step):
        left = jnp.full((8, B), flags[step, 0], jnp.int32) == 1
        for k in range(32):
            qa, qb = q[tile(k), 0:B], q[tile(k), B : 2 * B]
            q[tile(k), 0:B] = jnp.where(left, qb, qa)
            q[tile(k), B : 2 * B] = jnp.where(left, qa, qb)
        qhi[...], rest = split_rest(q[...])
        qmid[...], rest = split_rest(rest)
        qlo[...] = rest.astype(BF16)
        return left

    def multiply(block):
        high, low = split(block)
        qh = qhi[...]
        out = jnp.dot(high, qlo[...], preferred_element_type=F32)
        out = out + jnp.dot(low, qh, preferred_element_type=F32)
        out = out + jnp.dot(high, qmid[...], preferred_element_type=F32)
        return out + jnp.dot(high, qh, preferred_element_type=F32)

    def t_copy(c):
        return remote(t.at[at(c), :], tin.at[at(c), :], t_send.at[c], t_recv.at[c], fwd)

    def s_copy(c):
        return remote(s.at[at(c), :], sin.at[at(c - mid), :], s_send.at[c - mid], s_recv.at[c - mid], bwd)

    def u_copy(c):
        return remote(u.at[at(c), :], out_hbm.at[at(c), B : 2 * B], u_send.at[c], u_recv.at[c], fwd)

    def w_copy(step):
        if step == 0:
            return remote(w1.at[:, B : 2 * B], w1in, w_send.at[0], w_recv.at[0], fwd)
        return remote(w2.at[:, B : 2 * B], w2in, w_send.at[1], w_recv.at[1], fwd)

    d_copy = remote(d_out, d_in, d_send.at[0], d_recv.at[0], fwd)

    gram()
    pl.semaphore_wait(barrier, 17)
    reduce_all()
    for k in range(16):
        ra[tile(k), :] = full[spaced(k), :]
        rd[tile(k), :] = full[spaced(k, 2 * B), :]
    surplus = inner_rounds(counts[0], full.at[pl.ds(B, B), :], q, ra, rc, re, rd, ccol, scol)
    left = arrange(0)

    def rotate(c):
        y = multiply(x[at(c), :])
        s[at(c), :] = y[:, :B]
        t[at(c), :] = y[:, B:]

    def first_step(i, _):
        rotate(i)
        t_copy(i).start()
        rotate(mid + i)
        s_copy(mid + i).start()
        return 0

    lax.fori_loop(0, mid, first_step, 0)

    for k, second in enumerate(undo_moves(rd, surplus)):
        first = ra[tile(k), :]
        ra[tile(k), :] = jnp.where(left, second, first)
        d_out[tile(k), :] = jnp.where(left, first, second)
    d_copy.start()

    @pl.when(owner)
    def _():
        w1[...] = q[...]
        w_copy(0).start()

    @pl.when(jnp.logical_not(owner))
    def _():
        w1[...] = jnp.zeros_like(w1)

    @pl.when(jnp.logical_not(next_owner))
    def _():
        w1in[...] = jnp.zeros_like(w1in)

    hh[...] = jnp.zeros_like(hh)
    hl[...] = jnp.zeros_like(hl)

    def inner(one, two):
        one, two = jnp.concatenate(split(one), 1), jnp.concatenate(split(two), 1)
        return lax.dot_general(one, two, dims, preferred_element_type=F32)

    def meet(i, _):
        t_copy(i).wait_recv()
        hh[...] = hh[...] + inner(s[at(i), :], tin[at(i), :])
        s_copy(mid + i).wait_recv()
        hl[...] = hl[...] + inner(sin[at(i), :], t[at(mid + i), :])
        return 0

    lax.fori_loop(0, mid, meet, 0)
    for place, ref in enumerate((hh, hl)):
        mixed = ref[:B, B:] + ref[B:, :B]
        cross[place] = ref[:B, :B] + (mixed + ref[B:, B:])

    def send_rest():
        lax.fori_loop(mid, chunks, lambda c, _: (t_copy(c).start(), 0)[1], 0)

    reduce_cross(send_rest)
    d_copy.wait()
    for k in range(16):
        rd[tile(k), :] = d_in[tile(k), :]
    inner_rounds(counts[1], cross_full, q, ra, rc, re, rd, ccol, scol)
    arrange(1)

    def stay_copy(c):
        return pltpu.make_async_copy(v.at[at(c), :], out_hbm.at[at(c), 0:B], store_sem.at[c])

    def second_step(c, _):
        y = multiply(jnp.concatenate([s[at(c), :], tin[at(c), :]], 1))
        u[at(c), :] = y[:, B:]
        u_copy(c).start()
        v[at(c), :] = y[:, :B]
        stay_copy(c).start()
        return 0

    lax.fori_loop(0, mid, second_step, 0)

    def rest_of_second_step(c, _):
        t_copy(c).wait_recv()
        return second_step(c, _)

    lax.fori_loop(mid, chunks, rest_of_second_step, 0)

    @pl.when(next_owner)
    def _():
        w_copy(0).wait_recv()

    w2[...] = multiply(jnp.concatenate([w1[:, :B], w1in[...]], 1))
    w_out[:, :B] = w2[:, :B]

    @pl.when(jnp.logical_or(owner, next_owner))
    def _():
        w_copy(1).start()

    @pl.when(jnp.logical_not(jnp.logical_or(next_owner, third_owner)))
    def _():
        w_out[:, B:] = jnp.zeros((2 * B, B), F32)

    def finish(c, _):
        t_copy(c).wait_send()
        u_copy(c).wait_send()
        u_copy(c).wait_recv()
        stay_copy(c).wait()
        return 0

    lax.fori_loop(0, chunks, finish, 0)
    lax.fori_loop(mid, chunks, lambda c, _: (s_copy(c).wait_send(), 0)[1], 0)

    @pl.when(owner)
    def _():
        w_copy(0).wait_send()

    @pl.when(jnp.logical_or(owner, next_owner))
    def _():
        w_copy(1).wait_send()

    @pl.when(jnp.logical_or(next_owner, third_owner))
    def _():
        w_copy(1).wait_recv()
        w_out[:, B:] = w2in[...]


def per_device(jacobian, row_weight, col_scale, round_count, move_flag):
    scaled = jacobian * row_weight[:, None] * col_scale[None, :]
    rows = scaled.shape[0]
    chunks = rows // CH
    anywhere = pl.BlockSpec(memory_space=pl.ANY)
    vmem = pl.BlockSpec(memory_space=pltpu.VMEM)
    smem = pl.BlockSpec(memory_space=pltpu.SMEM)
    dma = pltpu.SemaphoreType.DMA
    square = pltpu.VMEM((B, B), F32)
    wide = pltpu.VMEM((2 * B, 2 * B), F32)
    narrow = pltpu.VMEM((2 * B, 2 * B), BF16)
    tall = pltpu.VMEM((2 * B, B), F32)
    column = pltpu.VMEM((rows, B), F32)
    return pl.pallas_call(
        body,
        out_shape=(
            jax.ShapeDtypeStruct((rows, 2 * B), F32),
            jax.ShapeDtypeStruct((2 * B, 2 * B), F32),
        ),
        in_specs=[smem, smem, anywhere],
        out_specs=(anywhere, vmem),
        scratch_shapes=[
            pltpu.VMEM((rows, 2 * B), F32), column, column, column, pltpu.VMEM((rows // 2, B), F32), column, column,
            pltpu.VMEM((3 * B, B), F32), wide, wide, wide, narrow, narrow, narrow,
            square, square, square, square, square, square,
            pltpu.VMEM((192, B), F32), pltpu.VMEM((7, 24, B), F32), pltpu.VMEM((3 * B, B), F32),
            pltpu.VMEM((2, B, B), F32), pltpu.VMEM((2, 64, B), F32),
            pltpu.VMEM((7, 8, B), F32), pltpu.VMEM((8, 8, B), F32), square, square, square,
            wide, tall, wide, tall,
            dma((chunks,)), dma((chunks,)), dma((chunks,)), dma((chunks,)),
            dma((chunks // 2,)), dma((chunks // 2,)), dma((chunks,)), dma((chunks,)),
            dma((4,)), dma((4,)), dma((2, 14)), dma((2, 14)), dma((8,)), dma((8,)), dma((2,)), dma((2,)), dma((1,)), dma((1,)),
        ],
        compiler_params=pltpu.CompilerParams(
            collective_id=0, has_side_effects=True, vmem_limit_bytes=56 * 2**20
        ),
        name="jacobi",
    )(round_count, move_flag, scaled)


def solution(mesh):
    in_specs = (P("rows", "blk"), P("rows"), P("blk"), P(), P(None, "blk"))
    out_specs = (P("rows", "blk"), P("rows", "blk"))
    return jax.shard_map(
        per_device, mesh=mesh, in_specs=in_specs, out_specs=out_specs, check_vma=False
    )
```

```python
import functools

import jax
import jax.numpy as jnp
from jax import lax
from jax.experimental import pallas as pl
from jax.experimental.pallas import tpu as pltpu
from jax.sharding import PartitionSpec as P

MESH = pl.DeviceIdType.MESH
B = 128
ROUNDS = 24
CH = 256
N_Y = 4
ROUND = 4
F32 = jnp.float32
BF16 = jnp.bfloat16


def split(x):
    high = x.astype(BF16)
    return high, (x - high.astype(F32)).astype(BF16)


def split_rest(x):
    high = x.astype(BF16)
    return high, x - high.astype(F32)


def rotation(first, second, cross, live):
    diff = second - first
    radius = jnp.sqrt(diff * diff + 4.0 * cross * cross)
    signs = jnp.where(diff >= 0.0, 1.0, -1.0)
    tangent = signs * 2.0 * cross / (jnp.abs(diff) + radius)
    cosine = 1.0 / jnp.sqrt(1.0 + tangent * tangent)
    sine = cosine * tangent
    return jnp.where(live, cosine, 1.0), jnp.where(live, sine, 0.0)


def tile(k):
    return pl.ds(8 * k, 8)


def spaced(k, start=0):
    return pl.ds(start + k, 8, stride=16)


def inner_rounds(count, cross, q, a, c, e, d, ccol, scol):
    count = jnp.full((8, B), count, jnp.int32)
    lane = lax.broadcasted_iota(jnp.int32, (8, B), 1)
    sub = lax.broadcasted_iota(jnp.int32, (8, B), 0)
    low = lane % 16
    on_diag = (lane // 16) == sub
    nxt = (lane + (B - 1)) % B
    nlow = nxt % 16
    on_next = (nxt // 16) == sub
    ccol[...] = jnp.transpose(cross[...])
    for k in range(16):
        c[tile(k), :] = cross[spaced(k), :]
        e[tile(k), :] = ccol[spaced(k), :]
    rows = lax.broadcasted_iota(jnp.int32, (2 * B, 2 * B), 0)
    cols = lax.broadcasted_iota(jnp.int32, (2 * B, 2 * B), 1)
    q[...] = (rows == cols).astype(F32)

    def pick(ref):
        acc = jnp.zeros((8, B), F32)
        for k in range(16):
            acc = jnp.where(low == k, ref[tile(k), :], acc)
        return total(jnp.where(on_diag, acc, 0.0))

    def total(x):
        return jnp.broadcast_to(jnp.sum(x, axis=0, keepdims=True), (8, B))

    def spread(cs, sn):
        ccol[...] = jnp.transpose(jnp.broadcast_to(cs[0:1], (B, B)))
        scol[...] = jnp.transpose(jnp.broadcast_to(sn[0:1], (B, B)))

    cs, sn = rotation(pick(a), pick(d), pick(c), 0 < count)
    spread(cs, sn)

    def one(index, carry):
        cs, sn = carry
        acc_a = acc_c = acc_d = jnp.zeros((8, B), F32)
        first = None
        for k in range(16):
            before = tile((k - 1) % 16)
            ck, sk = ccol[spaced(k), :], scol[spaced(k), :]
            ak, bk, ek, dk = a[tile(k), :], c[tile(k), :], e[tile(k), :], d[tile(k), :]
            a1 = ck * ak - sk * ek
            e1 = sk * ak + ck * ek
            b1 = ck * bk - sk * dk
            d1 = sk * bk + ck * dk
            a2 = a1 * cs - b1 * sn
            b2 = a1 * sn + b1 * cs
            e2 = e1 * cs - d1 * sn
            d2 = e1 * sn + d1 * cs
            acc_a = jnp.where(low == k, a2, acc_a)
            acc_d = jnp.where(low == k, d2, acc_d)
            acc_c = jnp.where(nlow == k, b2, acc_c)
            a[tile(k), :] = a2
            c[tile(k), :] = pltpu.roll(b2, B - 1, 1)
            d3 = pltpu.roll(d2, B - 1, 1)
            if k == 0:
                first = (e2, d3)
            else:
                e[before, :] = e2
                d[before, :] = d3
        e[tile(15), :] = pltpu.roll(first[0], 7, 0)
        d[tile(15), :] = pltpu.roll(first[1], 7, 0)
        diag_a = total(jnp.where(on_diag, acc_a, 0.0))
        diag_d = pltpu.roll(total(jnp.where(on_diag, acc_d, 0.0)), B - 1, 1)
        diag_c = pltpu.roll(total(jnp.where(on_next, acc_c, 0.0)), B - 1, 1)
        new = rotation(diag_a, diag_d, diag_c, index + 1 < count)
        for k in range(32):
            qa, qb = q[tile(k), 0:B], q[tile(k), B : 2 * B]
            q[tile(k), 0:B] = qa * cs - qb * sn
            q[tile(k), B : 2 * B] = pltpu.roll(qa * sn + qb * cs, B - 1, 1)
        spread(*new)
        return new

    lax.fori_loop(0, ROUNDS, one, (cs, sn))
    extra = ROUNDS - count
    surplus = [(extra >> bit) % 2 == 1 for bit in range(5)]
    for k in range(32):
        qb = q[tile(k), B : 2 * B]
        for bit in range(5):
            qb = jnp.where(surplus[bit], pltpu.roll(qb, 1 << bit, 1), qb)
        q[tile(k), B : 2 * B] = qb
    return surplus


def undo_moves(d, surplus):
    tiles = [d[tile(k), :] for k in range(16)]
    for bit in range(5):
        move = 1 << bit
        moved = []
        for k in range(16):
            value = pltpu.roll(tiles[(k - move) % 16], move, 1)
            moved.append(value if k >= move else pltpu.roll(value, 1, 0))
        tiles = [jnp.where(surplus[bit], new, old) for new, old in zip(moved, tiles)]
    return tiles


def body(
    counts, flags, weights_hbm, scales_hbm, x_hbm, out_hbm, w_out,
    weights, scales, x, s, t, tin, sin, u, v, r1, r2, g, hh, hl, q, qhi, qmid, qlo, ra, rc, re, rd, ccol, scol,
    half, piece, full, cross, cross_half, own_piece, far_piece, cross_full, d_out, d_in, w1, w1in, w2, w2in,
    small_sem, load_sem, store_sem, t_send, t_recv, s_send, s_recv, u_send, u_recv,
    r_send, r_recv, core_send, core_recv, z_send, z_recv, far_send, far_recv, w_send, w_recv, d_send, d_recv,
):
    row, blk = lax.axis_index("rows"), lax.axis_index("blk")
    n_blk = lax.axis_size("blk")
    z, core = row // 2, row % 2
    chunks = x.shape[0] // CH
    mid = chunks // 2
    next_blk = (blk + 1) % n_blk
    last_blk = (blk + n_blk - 1) % n_blk
    fwd, bwd = (row, next_blk), (row, last_blk)
    twin = (row + 1 - 2 * core, blk)
    peers = [(((z + i) % 8) * 2 + core, blk) for i in range(1, 8)]
    far = [(((z + i) % 8) * 2 + core, next_blk) for i in range(8)]
    far_from = [(((z + i) % 8) * 2 + core, last_blk) for i in range(8)]
    column = blk // N_Y * N_Y
    below = (row, column + (blk + N_Y - 1) % N_Y)
    above = (row, column + (blk + 1) % N_Y)
    last_hop = (row, (column + (blk + 2) % N_Y + 1) % n_blk)
    last_hop_from = (row, last_blk // N_Y * N_Y + (last_blk + 2) % N_Y)
    owner = row == blk
    next_owner = row == last_blk
    third_owner = row == (blk + n_blk - 2) % n_blk

    def at(c):
        return pl.ds(pl.multiple_of(c * CH, CH), CH)

    def load(c):
        return pltpu.make_async_copy(x_hbm.at[at(c), :], x.at[at(c), :], load_sem.at[c])

    small_loads = [
        pltpu.make_async_copy(weights_hbm, weights, small_sem.at[0]),
        pltpu.make_async_copy(scales_hbm, scales, small_sem.at[1]),
    ]
    for copy in small_loads:
        copy.start()
    lax.fori_loop(0, chunks, lambda c, _: (load(c).start(), 0)[1], 0)

    barrier = pltpu.get_barrier_semaphore()
    for device in [twin, fwd, above, last_hop_from] + peers + far_from:
        pl.semaphore_signal(barrier, inc=1, device_id=device, device_id_type=MESH)

    def remote(src, dst, send, recv, device):
        return pltpu.make_async_remote_copy(
            src_ref=src, dst_ref=dst, send_sem=send, recv_sem=recv, device_id=device, device_id_type=MESH
        )

    dims = (((0,), (0,)), ((), ()))

    def gram():
        hh[...] = jnp.zeros_like(hh)
        hl[...] = jnp.zeros_like(hl)

        for copy in small_loads:
            copy.wait()
        ccol[0 : weights.shape[0], :] = weights[...]
        ccol[weights.shape[0] :, :] = jnp.zeros((B - weights.shape[0], B), F32)
        scol[...] = jnp.transpose(ccol[...])
        lanes = lax.broadcasted_iota(jnp.int32, (B, B), 1)
        scale = jnp.concatenate([scales[0:1, :], scales[1:2, :]], 1)

        def add(c, acc):
            load(c).wait()
            parts = []
            for i in range(CH // B):
                column = jnp.where(lanes == c * (CH // B) + i, scol[...], 0.0)
                column = jnp.sum(column, axis=1, keepdims=True)
                rows = pl.ds(pl.multiple_of(c * CH + i * B, B), B)
                parts.append(x[rows, :] * column * scale)
                x[rows, :] = parts[-1]
            high, low = split(jnp.concatenate(parts, 0))
            both = lax.dot_general(high, jnp.concatenate([high, low], 1), dims, preferred_element_type=F32)
            small = low.astype(F32)
            hh[...] = hh[...] + both[:, : 2 * B]
            hl[...] = hl[...] + both[:, 2 * B :]
            return acc + jnp.sum((small * small).reshape(CH // 8, 8, 2 * B), axis=0)

        small = lax.fori_loop(0, chunks, add, jnp.zeros((8, 2 * B), F32))
        small = jnp.sum(small, axis=0, keepdims=True)
        rows = lax.broadcasted_iota(jnp.int32, (B, B), 0)
        cols = lax.broadcasted_iota(jnp.int32, (B, B), 1)
        for place, (i, j) in enumerate(((0, 0), (0, 1), (1, 1))):
            here, there = pl.ds(i * B, B), pl.ds(j * B, B)
            block = hh[here, there] + (hl[here, there] + jnp.transpose(hl[there, here]))
            if i == j:
                block = block + jnp.where(rows == cols, small[:, i * B : (i + 1) * B], 0.0)
            g[pl.ds(place * B, B), :] = block

    def exchange(index, src, dst):
        copy = remote(src, dst, core_send.at[index], core_recv.at[index], twin)
        copy.start()
        copy.wait()

    def share(step, ref, own):
        copies = []
        for i, peer in enumerate(peers):
            copies.append(remote(
                ref.at[own, :], ref.at[own, :], z_send.at[step, 7 + i], z_recv.at[step, 7 + i], peer
            ))
            copies[-1].start()
        for copy in copies:
            copy.wait()

    def reduce_all():
        mine = pl.ds(pl.multiple_of(core * 192, 8), 192)
        other = pl.ds(pl.multiple_of((1 - core) * 192, 8), 192)
        own = pl.ds(pl.multiple_of(core * 192 + z * 24, 8), 24)
        exchange(0, g.at[other, :], half.at[:, :])
        g[mine, :] = g[mine, :] + half[...]
        copies = []
        for i, peer in enumerate(peers):
            rows = pl.ds(pl.multiple_of(core * 192 + (peer[0] // 2) * 24, 8), 24)
            copies.append(remote(g.at[rows, :], piece.at[i], z_send.at[0, i], z_recv.at[0, i], peer))
            copies[-1].start()
        for copy in copies:
            copy.wait()
        total = g[own, :]
        for i in range(7):
            total = total + piece[i]
        full[own, :] = total
        share(0, full, own)
        exchange(1, full.at[mine, :], full.at[mine, :])

    def reduce_cross(started):
        mine = pl.ds(pl.multiple_of(core * 64, 8), 64)
        other = pl.ds(pl.multiple_of((1 - core) * 64, 8), 64)
        own = pl.ds(pl.multiple_of(core * 64 + z * 8, 8), 8)
        exchange(2, cross.at[:, other, :], cross_half)
        cross[:, mine, :] = cross[:, mine, :] + cross_half[...]
        copies = []
        for i, device in enumerate(far):
            rows = pl.ds(pl.multiple_of(core * 64 + (device[0] // 2) * 8, 8), 8)
            copies.append(remote(cross.at[1, rows, :], far_piece.at[i], far_send.at[i], far_recv.at[i], device))
            copies[-1].start()
        for i, peer in enumerate(peers):
            rows = pl.ds(pl.multiple_of(core * 64 + (peer[0] // 2) * 8, 8), 8)
            copies.append(remote(cross.at[0, rows, :], own_piece.at[i], z_send.at[1, i], z_recv.at[1, i], peer))
            copies[-1].start()
        started()
        for copy in copies:
            copy.wait()
        total = cross[0, own, :] + far_piece[0]
        for i in range(7):
            total = total + (own_piece[i] + far_piece[i + 1])
        cross_full[own, :] = total
        share(1, cross_full, own)
        exchange(3, cross_full.at[mine, :], cross_full.at[mine, :])

    def arrange(step):
        left = jnp.full((8, B), flags[0, step], jnp.int32) == 1
        for k in range(32):
            qa, qb = q[tile(k), 0:B], q[tile(k), B : 2 * B]
            q[tile(k), 0:B] = jnp.where(left, qb, qa)
            q[tile(k), B : 2 * B] = jnp.where(left, qa, qb)
        qhi[...], rest = split_rest(q[...])
        qmid[...], rest = split_rest(rest)
        qlo[...] = rest.astype(BF16)
        return left

    def multiply(block):
        high, low = split(block)
        qh = qhi[...]
        out = jnp.dot(high, qlo[...], preferred_element_type=F32)
        out = out + jnp.dot(low, qh, preferred_element_type=F32)
        out = out + jnp.dot(high, qmid[...], preferred_element_type=F32)
        return out + jnp.dot(high, qh, preferred_element_type=F32)

    def t_copy(c):
        return remote(t.at[at(c), :], tin.at[at(c), :], t_send.at[c], t_recv.at[c], fwd)

    def s_copy(c):
        return remote(s.at[at(c), :], sin.at[at(c - mid), :], s_send.at[c - mid], s_recv.at[c - mid], bwd)

    def u_copy(c):
        return remote(u.at[at(c), :], out_hbm.at[at(c), B : 2 * B], u_send.at[c], u_recv.at[c], fwd)

    def relay(hop, c):
        if hop == 0:
            return remote(u.at[at(c), :], r1.at[at(c), :], r_send.at[0, c], r_recv.at[0, c], below)
        if hop == 1:
            return remote(r1.at[at(c), :], r2.at[at(c), :], r_send.at[1, c], r_recv.at[1, c], below)
        return remote(r2.at[at(c), :], out_hbm.at[at(c), B : 2 * B], r_send.at[2, c], u_recv.at[c], last_hop)

    def w_copy(step):
        if step == 0:
            return remote(w1.at[:, B : 2 * B], w1in, w_send.at[0], w_recv.at[0], fwd)
        return remote(w2.at[:, B : 2 * B], w2in, w_send.at[1], w_recv.at[1], fwd)

    d_copy = remote(d_out, d_in, d_send.at[0], d_recv.at[0], fwd)

    gram()
    pl.semaphore_wait(barrier, 19)
    reduce_all()
    for k in range(16):
        ra[tile(k), :] = full[spaced(k), :]
        rd[tile(k), :] = full[spaced(k, 2 * B), :]
    surplus = inner_rounds(counts[0], full.at[pl.ds(B, B), :], q, ra, rc, re, rd, ccol, scol)
    left = arrange(0)

    def rotate(c):
        y = multiply(x[at(c), :])
        s[at(c), :] = y[:, :B]
        t[at(c), :] = y[:, B:]

    def first_step(i, _):
        rotate(i)
        t_copy(i).start()
        rotate(mid + i)
        s_copy(mid + i).start()
        return 0

    lax.fori_loop(0, mid, first_step, 0)

    for k, second in enumerate(undo_moves(rd, surplus)):
        first = ra[tile(k), :]
        ra[tile(k), :] = jnp.where(left, second, first)
        d_out[tile(k), :] = jnp.where(left, first, second)
    d_copy.start()

    @pl.when(owner)
    def _():
        w1[...] = q[...]
        w_copy(0).start()

    @pl.when(jnp.logical_not(owner))
    def _():
        w1[...] = jnp.zeros_like(w1)

    @pl.when(jnp.logical_not(next_owner))
    def _():
        w1in[...] = jnp.zeros_like(w1in)

    hh[...] = jnp.zeros_like(hh)
    hl[...] = jnp.zeros_like(hl)

    def inner(one, two):
        one, two = jnp.concatenate(split(one), 1), jnp.concatenate(split(two), 1)
        return lax.dot_general(one, two, dims, preferred_element_type=F32)

    def meet(i, _):
        t_copy(i).wait_recv()
        hh[...] = hh[...] + inner(s[at(i), :], tin[at(i), :])
        s_copy(mid + i).wait_recv()
        hl[...] = hl[...] + inner(sin[at(i), :], t[at(mid + i), :])
        return 0

    lax.fori_loop(0, mid, meet, 0)
    for place, ref in enumerate((hh, hl)):
        mixed = ref[:B, B:] + ref[B:, :B]
        cross[place] = ref[:B, :B] + (mixed + ref[B:, B:])

    def send_rest():
        lax.fori_loop(mid, chunks, lambda c, _: (t_copy(c).start(), 0)[1], 0)

    reduce_cross(send_rest)
    d_copy.wait()
    for k in range(16):
        rd[tile(k), :] = d_in[tile(k), :]
    inner_rounds(counts[1], cross_full, q, ra, rc, re, rd, ccol, scol)
    arrange(1)

    def stay_copy(c):
        return pltpu.make_async_copy(v.at[at(c), :], out_hbm.at[at(c), 0:B], store_sem.at[c])

    def second_step(c, send):
        y = multiply(jnp.concatenate([s[at(c), :], tin[at(c), :]], 1))
        u[at(c), :] = y[:, B:]
        send(c).start()
        v[at(c), :] = y[:, :B]
        stay_copy(c).start()

    def round_step(c, _):
        second_step(c, functools.partial(relay, 0))
        return 0

    def near_step(c, _):
        second_step(c, u_copy)
        return 0

    def late_step(c, _):
        t_copy(c).wait_recv()
        second_step(c, u_copy)
        return 0

    lax.fori_loop(0, ROUND, round_step, 0)
    lax.fori_loop(ROUND, mid, near_step, 0)
    lax.fori_loop(mid, chunks, late_step, 0)

    @pl.when(next_owner)
    def _():
        w_copy(0).wait_recv()

    w2[...] = multiply(jnp.concatenate([w1[:, :B], w1in[...]], 1))
    w_out[:, :B] = w2[:, :B]

    @pl.when(jnp.logical_or(owner, next_owner))
    def _():
        w_copy(1).start()

    @pl.when(jnp.logical_not(jnp.logical_or(next_owner, third_owner)))
    def _():
        w_out[:, B:] = jnp.zeros((2 * B, B), F32)

    for hop in (0, 1):

        def pass_on(c, _, hop=hop):
            relay(hop, c).wait_recv()
            relay(hop + 1, c).start()
            return 0

        lax.fori_loop(0, ROUND, pass_on, 0)

    def finish_round(c, _):
        for hop in range(3):
            relay(hop, c).wait_send()
        return 0

    lax.fori_loop(0, ROUND, finish_round, 0)
    lax.fori_loop(ROUND, chunks, lambda c, _: (u_copy(c).wait_send(), 0)[1], 0)

    def finish(c, _):
        t_copy(c).wait_send()
        u_copy(c).wait_recv()
        stay_copy(c).wait()
        return 0

    lax.fori_loop(0, chunks, finish, 0)
    lax.fori_loop(mid, chunks, lambda c, _: (s_copy(c).wait_send(), 0)[1], 0)

    @pl.when(owner)
    def _():
        w_copy(0).wait_send()

    @pl.when(jnp.logical_or(owner, next_owner))
    def _():
        w_copy(1).wait_send()

    @pl.when(jnp.logical_or(next_owner, third_owner))
    def _():
        w_copy(1).wait_recv()
        w_out[:, B:] = w2in[...]


def per_device(jacobian, row_weight, col_scale, round_count, move_flag):
    rows = jacobian.shape[0]
    chunks = rows // CH
    anywhere = pl.BlockSpec(memory_space=pl.ANY)
    vmem = pl.BlockSpec(memory_space=pltpu.VMEM)
    hbm = pl.BlockSpec(memory_space=pltpu.HBM)
    smem = pl.BlockSpec(memory_space=pltpu.SMEM)
    dma = pltpu.SemaphoreType.DMA
    square = pltpu.VMEM((B, B), F32)
    wide = pltpu.VMEM((2 * B, 2 * B), F32)
    narrow = pltpu.VMEM((2 * B, 2 * B), BF16)
    tall = pltpu.VMEM((2 * B, B), F32)
    column = pltpu.VMEM((rows, B), F32)
    relayed = pltpu.VMEM((ROUND * CH, B), F32)
    return pl.pallas_call(
        body,
        out_shape=(
            jax.ShapeDtypeStruct((rows, 2 * B), F32),
            jax.ShapeDtypeStruct((2 * B, 2 * B), F32),
        ),
        in_specs=[smem, smem, hbm, hbm, hbm],
        out_specs=(anywhere, vmem),
        scratch_shapes=[
            pltpu.VMEM((rows // B, B), F32), pltpu.VMEM((2, B), F32),
            pltpu.VMEM((rows, 2 * B), F32), column, column, column, pltpu.VMEM((rows // 2, B), F32), column, column,
            relayed, relayed,
            pltpu.VMEM((3 * B, B), F32), wide, wide, wide, narrow, narrow, narrow,
            square, square, square, square, square, square,
            pltpu.VMEM((192, B), F32), pltpu.VMEM((7, 24, B), F32), pltpu.VMEM((3 * B, B), F32),
            pltpu.VMEM((2, B, B), F32), pltpu.VMEM((2, 64, B), F32),
            pltpu.VMEM((7, 8, B), F32), pltpu.VMEM((8, 8, B), F32), square, square, square,
            wide, tall, wide, tall,
            dma((2,)), dma((chunks,)), dma((chunks,)), dma((chunks,)), dma((chunks,)),
            dma((chunks // 2,)), dma((chunks // 2,)), dma((chunks,)), dma((chunks,)),
            dma((3, ROUND)), dma((2, ROUND)), dma((4,)), dma((4,)), dma((2, 14)), dma((2, 14)), dma((8,)), dma((8,)), dma((2,)), dma((2,)), dma((1,)), dma((1,)),
        ],
        compiler_params=pltpu.CompilerParams(
            collective_id=0, has_side_effects=True, vmem_limit_bytes=56 * 2**20
        ),
        name="jacobi",
    )(round_count, move_flag.T, row_weight.reshape(rows // B, B), col_scale.reshape(2, B), jacobian)


def solution(mesh):
    in_specs = (P("rows", "blk"), P("rows"), P("blk"), P(), P(None, "blk"))
    out_specs = (P("rows", "blk"), P("rows", "blk"))
    return jax.shard_map(
        per_device, mesh=mesh, in_specs=in_specs, out_specs=out_specs, check_vma=False
    )
```

```python
import functools

import jax
import jax.numpy as jnp
from jax import lax
from jax.experimental import pallas as pl
from jax.experimental.pallas import tpu as pltpu
from jax.sharding import PartitionSpec as P

MESH = pl.DeviceIdType.MESH
B = 128
ROUNDS = 24
CH = 256
N_Y = 4
ROUND = 3
AHEAD = 4
EARLY = 4
F32 = jnp.float32
BF16 = jnp.bfloat16


def split(x):
    high = x.astype(BF16)
    return high, (x - high.astype(F32)).astype(BF16)


def split_rest(x):
    high = x.astype(BF16)
    return high, x - high.astype(F32)


def rotation(first, second, cross, live):
    diff = second - first
    inverse = lax.rsqrt(diff * diff + 4.0 * cross * cross)
    square = 0.5 + 0.5 * (jnp.abs(diff) * inverse)
    scale = lax.rsqrt(square)
    sine = jnp.where(diff >= 0.0, cross, -cross) * inverse * scale
    return jnp.where(live, square * scale, 1.0), jnp.where(live, sine, 0.0)


def tile(k):
    return pl.ds(8 * k, 8)


def spaced(k, start=0):
    return pl.ds(start + k, 8, stride=16)


def inner_rounds(count, cross, out, q, upper, lower, a, c, e, d, ccol, scol):
    count = jnp.full((8, B), count, jnp.int32)
    lane = lax.broadcasted_iota(jnp.int32, (8, B), 1)
    sub = lax.broadcasted_iota(jnp.int32, (8, B), 0)

    def band(distance):
        row = (lane + (B - distance)) % B
        return row % 16, (row // 16) == sub

    bands = [band(distance) for distance in range(3)]

    def left(x, distance=1):
        return pltpu.roll(x, B - distance, 1)

    def total(x, distance):
        x = jnp.where(bands[distance][1], x, 0.0)
        return jnp.broadcast_to(jnp.sum(x, axis=0, keepdims=True), (8, B))

    def pick(ref, distance):
        acc = jnp.zeros((8, B), F32)
        for k in range(16):
            acc = jnp.where(bands[distance][0] == k, ref[tile(k), :], acc)
        return left(total(acc, distance), distance) if distance else total(acc, 0)

    def spread(cs, sn, place):
        for k in range(16):
            own = bands[0][1] & (bands[0][0] == k)
            ccol[place, tile(k), :] = jnp.broadcast_to(jnp.sum(jnp.where(own, cs, 0.0), axis=1, keepdims=True), (8, B))
            scol[place, tile(k), :] = jnp.broadcast_to(jnp.sum(jnp.where(own, sn, 0.0), axis=1, keepdims=True), (8, B))

    ccol[0] = jnp.transpose(cross[...])
    for k in range(16):
        c[tile(k), :] = cross[spaced(k), :]
        e[tile(k), :] = ccol[0, spaced(k), :]
    wide_lane = lax.broadcasted_iota(jnp.int32, (8, 2 * B), 1)
    wide_row = 16 * lax.broadcasted_iota(jnp.int32, (8, 2 * B), 0)
    for k in range(16):
        upper[tile(k), :] = (wide_lane == wide_row + k).astype(F32)
        lower[tile(k), :] = (wide_lane == wide_row + (B + k)).astype(F32)
    diag_a, diag_d, diag_c = pick(a, 0), pick(d, 0), pick(c, 0)
    near = pick(a, 1), pick(c, 1), pick(e, 1), pick(d, 1)
    cs, sn = rotation(diag_a, diag_d, diag_c, 0 < count)
    spread(cs, sn, 0)

    def one(index, place, carry):
        cs, sn, diag_a, diag_d, diag_c, near_a, near_c, near_e, near_d = carry
        new_c = left(sn) * (cs * near_a - sn * near_e) + left(cs) * (cs * near_c - sn * near_d)
        new_a = cs * (cs * diag_a - sn * diag_c) - sn * (cs * diag_c - sn * diag_d)
        new_d = left(sn * (sn * diag_a + cs * diag_c) + cs * (sn * diag_c + cs * diag_d))
        new = rotation(new_a, new_d, new_c, index + 1 < count)
        spread(*new, 1 - place)
        acc_a = acc_c = acc_d = acc_e = jnp.zeros((8, B), F32)
        first = None
        for k in range(16):
            before = tile((k - 1) % 16)
            ck, sk = ccol[place, tile(k), :], scol[place, tile(k), :]
            ak, bk, ek, dk = a[tile(k), :], c[tile(k), :], e[tile(k), :], d[tile(k), :]
            cw, sw = jnp.concatenate([ck, ck], 1), jnp.concatenate([sk, sk], 1)
            qu, ql = upper[tile(k), :], lower[tile(k), :]
            upper[tile(k), :] = cw * qu - sw * ql
            q2 = sw * qu + cw * ql
            a1 = ck * ak - sk * ek
            e1 = sk * ak + ck * ek
            b1 = ck * bk - sk * dk
            d1 = sk * bk + ck * dk
            a2 = a1 * cs - b1 * sn
            b2 = a1 * sn + b1 * cs
            e2 = e1 * cs - d1 * sn
            d2 = e1 * sn + d1 * cs
            acc_a = jnp.where(bands[1][0] == k, a2, acc_a)
            acc_c = jnp.where(bands[2][0] == k, b2, acc_c)
            acc_e = jnp.where(bands[0][0] == k, e2, acc_e)
            acc_d = jnp.where(bands[1][0] == k, d2, acc_d)
            a[tile(k), :] = a2
            c[tile(k), :] = left(b2)
            d3 = left(d2)
            if k == 0:
                first = (e2, d3, q2)
            else:
                lower[before, :] = q2
                e[before, :] = e2
                d[before, :] = d3
        e[tile(15), :] = pltpu.roll(first[0], 7, 0)
        d[tile(15), :] = pltpu.roll(first[1], 7, 0)
        lower[tile(15), :] = pltpu.roll(first[2], 7, 0)
        near = (left(total(acc_a, 1)), left(total(acc_c, 2), 2), left(total(acc_e, 0)), left(total(acc_d, 1), 2))
        return (*new, new_a, new_d, new_c, *near)

    def two(index, carry):
        return one(2 * index + 1, 1, one(2 * index, 0, carry))

    lax.fori_loop(0, ROUNDS // 2, two, (cs, sn, diag_a, diag_d, diag_c, *near))
    extra = ROUNDS - count
    surplus = [(extra >> bit) % 2 == 1 for bit in range(5)]
    tiles = [lower[tile(k), :] for k in range(16)]
    for bit in range(5):
        tiles = undo_rows(tiles, bit, surplus[bit])
    for k in range(16):
        q[spaced(k), :] = tiles[k][:, :B]
        q[spaced(k, B), :] = tiles[k][:, B:]
    out[:B, B:], out[B:, B:] = jnp.transpose(q[:B, :]), jnp.transpose(q[B:, :])
    for k in range(16):
        q[spaced(k), :] = upper[tile(k), :B]
        q[spaced(k, B), :] = upper[tile(k), B:]
    out[:B, :B], out[B:, :B] = jnp.transpose(q[:B, :]), jnp.transpose(q[B:, :])
    return surplus


def undo_rows(tiles, bit, on):
    move = 1 << bit
    moved = []
    for k in range(16):
        value = tiles[(k - move) % 16]
        moved.append(value if k >= move else pltpu.roll(value, 1, 0))
    return [jnp.where(on[0:1, 0:1], new, old) for new, old in zip(moved, tiles)]


def undo_moves(d, surplus):
    tiles = [d[tile(k), :] for k in range(16)]
    for bit in range(5):
        move = 1 << bit
        moved = []
        for k in range(16):
            value = pltpu.roll(tiles[(k - move) % 16], move, 1)
            moved.append(value if k >= move else pltpu.roll(value, 1, 0))
        tiles = [jnp.where(surplus[bit], new, old) for new, old in zip(moved, tiles)]
    return tiles


def body(
    counts, flags, weights_hbm, scales_hbm, x_hbm, out_hbm, w_out,
    x_in, s_in, t_far, q_in0, q_in1, p0a, p0b, p0c, p1a, p1b, p1c,
    x_send, x_recv, f_send, f_recv, q_send, q_recv, far_sem,
    weights, scales, x, s, t, tin, sin, u, v, r1, r2, g, hh, hl, q, qn, qa, qb, qhi, qmid, qlo, ra, rc, re, rd, ccol, scol,
    half, piece, full, cross, cross_half, own_piece, far_piece, cross_full, d_out, d_in, w1, w1in, w2, w2in,
    small_sem, load_sem, store_sem, t_send, t_recv, s_send, s_recv, u_send, u_recv,
    r_send, r_recv, core_send, core_recv, z_send, z_recv, far_send, far_recv, w_send, w_recv, d_send, d_recv,
):
    q_in, q_parts = (q_in0, q_in1), ((p0a, p0b, p0c), (p1a, p1b, p1c))
    row, blk = lax.axis_index("rows"), lax.axis_index("blk")
    n_blk = lax.axis_size("blk")
    z, core = row // 2, row % 2
    chunks = x.shape[0] // CH
    mid = (AHEAD + chunks) // 2
    next_blk = (blk + 1) % n_blk
    last_blk = (blk + n_blk - 1) % n_blk
    fwd, bwd = (row, next_blk), (row, last_blk)
    twin = (row + 1 - 2 * core, blk)
    peers = [(((z + i) % 8) * 2 + core, blk) for i in range(1, 8)]
    far = [(((z + i) % 8) * 2 + core, next_blk) for i in range(8)]
    far_from = [(((z + i) % 8) * 2 + core, last_blk) for i in range(8)]
    column = blk // N_Y * N_Y
    below = (row, column + (blk + N_Y - 1) % N_Y)
    above = (row, column + (blk + 1) % N_Y)
    last_hop = (row, (column + (blk + 2) % N_Y + 1) % n_blk)
    last_hop_from = (row, last_blk // N_Y * N_Y + (last_blk + 2) % N_Y)
    owner = row == blk
    next_owner = row == last_blk
    third_owner = row == (blk + n_blk - 2) % n_blk

    def at(c):
        return pl.ds(pl.multiple_of(c * CH, CH), CH)

    def load(c):
        return pltpu.make_async_copy(x_hbm.at[at(c), :], x.at[at(c), :], load_sem.at[c])

    small_loads = [
        pltpu.make_async_copy(weights_hbm, weights, small_sem.at[0]),
        pltpu.make_async_copy(scales_hbm, scales, small_sem.at[1]),
    ]
    for copy in small_loads:
        copy.start()
    lax.fori_loop(0, chunks, lambda c, _: (load(c).start(), 0)[1], 0)

    barrier = pltpu.get_barrier_semaphore()
    for device in [twin, fwd, above, last_hop_from] + peers + far_from:
        pl.semaphore_signal(barrier, inc=1, device_id=device, device_id_type=MESH)

    pl.semaphore_wait(barrier, 19)

    def remote(src, dst, send, recv, device):
        return pltpu.make_async_remote_copy(
            src_ref=src, dst_ref=dst, send_sem=send, recv_sem=recv, device_id=device, device_id_type=MESH
        )

    dims = (((0,), (0,)), ((), ()))

    def gram():
        hh[...] = jnp.zeros_like(hh)
        hl[...] = jnp.zeros_like(hl)

        for copy in small_loads:
            copy.wait()
        ccol[0, 0 : weights.shape[0], :] = weights[...]
        ccol[0, weights.shape[0] :, :] = jnp.zeros((B - weights.shape[0], B), F32)
        scol[0] = jnp.transpose(ccol[0])
        lanes = lax.broadcasted_iota(jnp.int32, (B, B), 1)
        scale = jnp.concatenate([scales[0:1, :], scales[1:2, :]], 1)

        def add(ahead, c, acc):
            load(c).wait()
            parts = []
            for i in range(CH // B):
                column = jnp.where(lanes == c * (CH // B) + i, scol[0], 0.0)
                column = jnp.sum(column, axis=1, keepdims=True)
                rows = pl.ds(pl.multiple_of(c * CH + i * B, B), B)
                parts.append(x[rows, :] * column * scale)
                x[rows, :] = parts[-1]
            if ahead:
                x_copy(c).start()
            high, low = split(jnp.concatenate(parts, 0))
            both = lax.dot_general(high, jnp.concatenate([high, low], 1), dims, preferred_element_type=F32)
            small = low.astype(F32)
            hh[...] = hh[...] + both[:, : 2 * B]
            hl[...] = hl[...] + both[:, 2 * B :]
            return acc + jnp.sum((small * small).reshape(CH // 8, 8, 2 * B), axis=0)

        small = lax.fori_loop(0, EARLY, functools.partial(add, True), jnp.zeros((8, 2 * B), F32))
        small = lax.fori_loop(EARLY, chunks, functools.partial(add, False), small)
        small = jnp.sum(small, axis=0, keepdims=True)
        rows = lax.broadcasted_iota(jnp.int32, (B, B), 0)
        cols = lax.broadcasted_iota(jnp.int32, (B, B), 1)
        for place, (i, j) in enumerate(((0, 0), (0, 1), (1, 1))):
            here, there = pl.ds(i * B, B), pl.ds(j * B, B)
            block = hh[here, there] + (hl[here, there] + jnp.transpose(hl[there, here]))
            if i == j:
                block = block + jnp.where(rows == cols, small[:, i * B : (i + 1) * B], 0.0)
            g[pl.ds(place * B, B), :] = block

    def exchange(index, src, dst):
        copy = remote(src, dst, core_send.at[index], core_recv.at[index], twin)
        copy.start()
        copy.wait()

    def share_start(step, ref, own):
        copies = []
        for i, peer in enumerate(peers):
            copies.append(remote(
                ref.at[own, :], ref.at[own, :], z_send.at[step, 7 + i], z_recv.at[step, 7 + i], peer
            ))
            copies[-1].start()
        return copies

    def share(step, ref, own):
        for copy in share_start(step, ref, own):
            copy.wait()

    def reduce_all():
        mine = pl.ds(pl.multiple_of(core * 192, 8), 192)
        other = pl.ds(pl.multiple_of((1 - core) * 192, 8), 192)
        own = pl.ds(pl.multiple_of(core * 192 + z * 24, 8), 24)
        exchange(0, g.at[other, :], half.at[:, :])
        g[mine, :] = g[mine, :] + half[...]
        copies = []
        for i, peer in enumerate(peers):
            rows = pl.ds(pl.multiple_of(core * 192 + (peer[0] // 2) * 24, 8), 24)
            copies.append(remote(g.at[rows, :], piece.at[i], z_send.at[0, i], z_recv.at[0, i], peer))
            copies[-1].start()
        for copy in copies:
            copy.wait()
        total = g[own, :]
        for i in range(7):
            total = total + piece[i]
        full[own, :] = total
        share(0, full, own)
        exchange(1, full.at[mine, :], full.at[mine, :])

    def reduce_cross(started):
        mine = pl.ds(pl.multiple_of(core * 64, 8), 64)
        other = pl.ds(pl.multiple_of((1 - core) * 64, 8), 64)
        own = pl.ds(pl.multiple_of(core * 64 + z * 8, 8), 8)
        exchange(2, cross.at[:, other, :], cross_half)
        cross[:, mine, :] = cross[:, mine, :] + cross_half[...]
        copies = []
        for i, device in enumerate(far):
            rows = pl.ds(pl.multiple_of(core * 64 + (device[0] // 2) * 8, 8), 8)
            copies.append(remote(cross.at[1, rows, :], far_piece.at[i], far_send.at[i], far_recv.at[i], device))
            copies[-1].start()
        for i, peer in enumerate(peers):
            rows = pl.ds(pl.multiple_of(core * 64 + (peer[0] // 2) * 8, 8), 8)
            copies.append(remote(cross.at[0, rows, :], own_piece.at[i], z_send.at[1, i], z_recv.at[1, i], peer))
            copies[-1].start()
        started()
        for copy in copies:
            copy.wait()
        total = cross[0, own, :] + far_piece[0]
        for i in range(7):
            total = total + (own_piece[i] + far_piece[i + 1])
        cross_full[own, :] = total
        share(1, cross_full, own)
        exchange(3, cross_full.at[mine, :], cross_full.at[mine, :])

    def arrange(step):
        left = jnp.full((8, B), flags[0, step], jnp.int32) == 1
        for k in range(32):
            qa, qb = q[tile(k), 0:B], q[tile(k), B : 2 * B]
            q[tile(k), 0:B] = jnp.where(left, qb, qa)
            q[tile(k), B : 2 * B] = jnp.where(left, qa, qb)
        three(q, qhi, qmid, qlo)
        return left

    def three(source, high, middle, low):
        high[...], rest = split_rest(source[...])
        middle[...], rest = split_rest(rest)
        low[...] = rest.astype(BF16)

    def q_copy(step):
        own = pl.ds(pl.multiple_of(core * B + z * 16, 16), 16)
        source = q.at[own, :] if step == 0 else q.at[own, B : 2 * B]
        return remote(source, q_in[step].at[own, :], q_send.at[step], q_recv.at[step], fwd)

    def gather_begin(step):
        own = pl.ds(pl.multiple_of(core * B + z * 16, 16), 16)
        q_copy(step).wait()
        return share_start(2 + step, q_in[step], own)

    def gather_middle(step, copies):
        mine = pl.ds(pl.multiple_of(core * B, B), B)
        for copy in copies:
            copy.wait()
        last = remote(
            q_in[step].at[mine, :], q_in[step].at[mine, :], core_send.at[4 + step], core_recv.at[4 + step], twin
        )
        last.start()
        return last

    def gather_end(step, last):
        last.wait()
        three(q_in[step], *q_parts[step])

    def x_copy(c):
        return remote(x.at[at(c), :], x_in.at[at(c), :], x_send.at[c], x_recv.at[c], fwd)

    def far_copy(c):
        return remote(tin.at[at(c), :], t_far.at[at(c), :], f_send.at[c], f_recv.at[c], fwd)

    def multiply(block, parts=(qhi, qmid, qlo)):
        high, low = split(block)
        qh = parts[0][...]
        out = jnp.dot(high, parts[2][...], preferred_element_type=F32)
        out = out + jnp.dot(low, qh, preferred_element_type=F32)
        out = out + jnp.dot(high, parts[1][...], preferred_element_type=F32)
        return out + jnp.dot(high, qh, preferred_element_type=F32)

    def t_copy(c):
        return remote(t.at[at(c), :], tin.at[at(c), :], t_send.at[c], t_recv.at[c], fwd)

    def s_copy(c):
        return remote(s.at[at(c), :], sin.at[at(c - mid), :], s_send.at[c - mid], s_recv.at[c - mid], bwd)

    def u_copy(c):
        return remote(u.at[at(c), :], out_hbm.at[at(c), B : 2 * B], u_send.at[c], u_recv.at[c], fwd)

    def relay(hop, c):
        i = c - AHEAD
        if hop == 0:
            return remote(u.at[at(c), :], r1.at[at(i), :], r_send.at[0, i], r_recv.at[0, i], below)
        if hop == 1:
            return remote(r1.at[at(i), :], r2.at[at(i), :], r_send.at[1, i], r_recv.at[1, i], below)
        return remote(r2.at[at(i), :], out_hbm.at[at(c), B : 2 * B], r_send.at[2, i], u_recv.at[c], last_hop)

    def w_copy(step):
        if step == 0:
            return remote(w1.at[:, B : 2 * B], w1in, w_send.at[0], w_recv.at[0], fwd)
        return remote(w2.at[:, B : 2 * B], w2in, w_send.at[1], w_recv.at[1], fwd)

    d_copy = remote(d_out, d_in, d_send.at[0], d_recv.at[0], fwd)

    gram()
    reduce_all()
    lax.fori_loop(EARLY, AHEAD, lambda c, _: (x_copy(c).start(), 0)[1], 0)
    for k in range(16):
        ra[tile(k), :] = full[spaced(k), :]
        rd[tile(k), :] = full[spaced(k, 2 * B), :]
    surplus = inner_rounds(counts[0], full.at[pl.ds(B, B), :], q, qn, qa, qb, ra, rc, re, rd, ccol, scol)
    left = arrange(0)

    def rotate(c):
        y = multiply(x[at(c), :])
        s[at(c), :] = y[:, :B]
        t[at(c), :] = y[:, B:]

    def first_step(i, _):
        rotate(AHEAD + i)
        t_copy(AHEAD + i).start()
        rotate(mid + i)
        s_copy(mid + i).start()
        return 0

    q_copy(0).start()
    lax.fori_loop(0, mid - AHEAD, first_step, 0)

    def rotate_own(c, _):
        s[at(c), :] = multiply(x[at(c), :])[:, :B]
        return 0

    lax.fori_loop(0, AHEAD, rotate_own, 0)

    for k, second in enumerate(undo_moves(rd, surplus)):
        first = ra[tile(k), :]
        ra[tile(k), :] = jnp.where(left, second, first)
        d_out[tile(k), :] = jnp.where(left, first, second)
    d_copy.start()

    @pl.when(owner)
    def _():
        w1[...] = q[...]
        w_copy(0).start()

    @pl.when(jnp.logical_not(owner))
    def _():
        w1[...] = jnp.zeros_like(w1)

    @pl.when(jnp.logical_not(next_owner))
    def _():
        w1in[...] = jnp.zeros_like(w1in)

    hh[...] = jnp.zeros_like(hh)
    hl[...] = jnp.zeros_like(hl)

    def inner(one, two):
        one, two = jnp.concatenate(split(one), 1), jnp.concatenate(split(two), 1)
        return lax.dot_general(one, two, dims, preferred_element_type=F32)

    pending = gather_begin(0)

    def meet_own(c, _):
        x_copy(c).wait_recv()
        y = multiply(x_in[at(c), :], q_parts[0])
        s_in[at(c), :] = y[:, :B]
        tin[at(c), :] = y[:, B:]
        hh[...] = hh[...] + inner(s[at(c), :], y[:, B:])
        return 0

    def meet(i, _):
        c = AHEAD + i
        t_copy(c).wait_recv()
        hh[...] = hh[...] + inner(s[at(c), :], tin[at(c), :])
        s_copy(mid + i).wait_recv()
        hl[...] = hl[...] + inner(sin[at(i), :], t[at(mid + i), :])
        return 0

    pairs = mid - AHEAD
    lax.fori_loop(0, pairs // 3, meet, 0)
    pending = gather_middle(0, pending)
    lax.fori_loop(pairs // 3, pairs * 2 // 3, meet, 0)
    gather_end(0, pending)
    lax.fori_loop(0, AHEAD, meet_own, 0)
    lax.fori_loop(pairs * 2 // 3, pairs, meet, 0)
    for place, ref in enumerate((hh, hl)):
        mixed = ref[:B, B:] + ref[B:, :B]
        cross[place] = ref[:B, :B] + (mixed + ref[B:, B:])

    def send_rest():
        lax.fori_loop(mid, chunks, lambda c, _: (t_copy(c).start(), 0)[1], 0)
        lax.fori_loop(0, AHEAD, lambda c, _: (far_copy(c).start(), 0)[1], 0)

    reduce_cross(send_rest)
    d_copy.wait()
    for k in range(16):
        rd[tile(k), :] = d_in[tile(k), :]
    inner_rounds(counts[1], cross_full, q, qn, qa, qb, ra, rc, re, rd, ccol, scol)
    arrange(1)
    q_copy(1).start()

    def stay_copy(c):
        return pltpu.make_async_copy(v.at[at(c), :], out_hbm.at[at(c), 0:B], store_sem.at[c])

    def second_step(c, send):
        y = multiply(jnp.concatenate([s[at(c), :], tin[at(c), :]], 1))
        u[at(c), :] = y[:, B:]
        send(c).start()
        v[at(c), :] = y[:, :B]
        stay_copy(c).start()

    def round_step(c, _):
        second_step(c, functools.partial(relay, 0))
        return 0

    def near_step(c, _):
        second_step(c, u_copy)
        return 0

    def late_step(c, _):
        t_copy(c).wait_recv()
        second_step(c, u_copy)
        return 0

    def own_step(c, _):
        y = multiply(jnp.concatenate([s[at(c), :], tin[at(c), :]], 1))
        v[at(c), :] = y[:, :B]
        stay_copy(c).start()
        return 0

    def far_store(c):
        return pltpu.make_async_copy(u.at[at(c), :], out_hbm.at[at(c), B : 2 * B], far_sem.at[c])

    def far_step(c, _):
        far_copy(c).wait_recv()
        u[at(c), :] = multiply(jnp.concatenate([s_in[at(c), :], t_far[at(c), :]], 1), q_parts[1])
        far_store(c).start()
        return 0

    lax.fori_loop(AHEAD, AHEAD + ROUND, round_step, 0)
    lax.fori_loop(AHEAD + ROUND, mid, near_step, 0)
    lax.fori_loop(mid, chunks, late_step, 0)
    lax.fori_loop(0, AHEAD, own_step, 0)
    pending = gather_begin(1)

    @pl.when(next_owner)
    def _():
        w_copy(0).wait_recv()

    w2[...] = multiply(jnp.concatenate([w1[:, :B], w1in[...]], 1))
    w_out[:, :B] = w2[:, :B]

    @pl.when(jnp.logical_or(owner, next_owner))
    def _():
        w_copy(1).start()

    @pl.when(jnp.logical_not(jnp.logical_or(next_owner, third_owner)))
    def _():
        w_out[:, B:] = jnp.zeros((2 * B, B), F32)

    for hop in (0, 1):

        def pass_on(c, _, hop=hop):
            relay(hop, c).wait_recv()
            relay(hop + 1, c).start()
            return 0

        lax.fori_loop(AHEAD, AHEAD + ROUND, pass_on, 0)
        if hop == 0:
            pending = gather_middle(1, pending)

    gather_end(1, pending)
    lax.fori_loop(0, AHEAD, far_step, 0)

    def finish_round(c, _):
        for hop in range(3):
            relay(hop, c).wait_send()
        return 0

    lax.fori_loop(AHEAD, AHEAD + ROUND, finish_round, 0)
    lax.fori_loop(AHEAD + ROUND, chunks, lambda c, _: (u_copy(c).wait_send(), 0)[1], 0)

    def finish(c, _):
        t_copy(c).wait_send()
        u_copy(c).wait_recv()
        stay_copy(c).wait()
        return 0

    def finish_own(c, _):
        x_copy(c).wait_send()
        far_copy(c).wait_send()
        far_store(c).wait()
        stay_copy(c).wait()
        return 0

    lax.fori_loop(AHEAD, chunks, finish, 0)
    lax.fori_loop(0, AHEAD, finish_own, 0)
    lax.fori_loop(mid, chunks, lambda c, _: (s_copy(c).wait_send(), 0)[1], 0)

    @pl.when(owner)
    def _():
        w_copy(0).wait_send()

    @pl.when(jnp.logical_or(owner, next_owner))
    def _():
        w_copy(1).wait_send()

    @pl.when(jnp.logical_or(next_owner, third_owner))
    def _():
        w_copy(1).wait_recv()
        w_out[:, B:] = w2in[...]


def per_device(jacobian, row_weight, col_scale, round_count, move_flag):
    rows = jacobian.shape[0]
    chunks = rows // CH
    anywhere = pl.BlockSpec(memory_space=pl.ANY)
    vmem = pl.BlockSpec(memory_space=pltpu.VMEM)
    hbm = pl.BlockSpec(memory_space=pltpu.HBM)
    smem = pl.BlockSpec(memory_space=pltpu.SMEM)
    dma = pltpu.SemaphoreType.DMA
    square = pltpu.VMEM((B, B), F32)
    double = pltpu.VMEM((2, B, B), F32)
    wide = pltpu.VMEM((2 * B, 2 * B), F32)
    narrow = pltpu.VMEM((2 * B, 2 * B), BF16)
    tall = pltpu.VMEM((2 * B, B), F32)
    flat = pltpu.VMEM((B, 2 * B), F32)
    column = pltpu.VMEM((rows, B), F32)
    ahead = pltpu.VMEM((AHEAD * CH, B), F32)
    thin = pltpu.VMEM((2 * B, B), BF16)
    relayed = pltpu.VMEM((ROUND * CH, B), F32)
    return pl.pallas_call(
        body,
        out_shape=(
            jax.ShapeDtypeStruct((rows, 2 * B), F32),
            jax.ShapeDtypeStruct((2 * B, 2 * B), F32),
        ),
        in_specs=[smem, smem, hbm, hbm, hbm],
        out_specs=(anywhere, vmem),
        scratch_shapes=[
            pltpu.VMEM((AHEAD * CH, 2 * B), F32), ahead, ahead, wide, tall,
            narrow, narrow, narrow, thin, thin, thin,
            dma((AHEAD,)), dma((AHEAD,)), dma((AHEAD,)), dma((AHEAD,)), dma((2,)), dma((2,)), dma((AHEAD,)),
            pltpu.VMEM((rows // B, B), F32), pltpu.VMEM((2, B), F32),
            pltpu.VMEM((rows, 2 * B), F32), column, column, column, pltpu.VMEM((rows // 2, B), F32), column, column,
            relayed, relayed,
            pltpu.VMEM((3 * B, B), F32), wide, wide, wide, tall, flat, flat, narrow, narrow, narrow,
            square, square, square, square, double, double,
            pltpu.VMEM((192, B), F32), pltpu.VMEM((7, 24, B), F32), pltpu.VMEM((3 * B, B), F32),
            pltpu.VMEM((2, B, B), F32), pltpu.VMEM((2, 64, B), F32),
            pltpu.VMEM((7, 8, B), F32), pltpu.VMEM((8, 8, B), F32), square, square, square,
            wide, tall, wide, tall,
            dma((2,)), dma((chunks,)), dma((chunks,)), dma((chunks,)), dma((chunks,)),
            dma((chunks // 2,)), dma((chunks // 2,)), dma((chunks,)), dma((chunks,)),
            dma((3, ROUND)), dma((2, ROUND)), dma((6,)), dma((6,)), dma((4, 14)), dma((4, 14)), dma((8,)), dma((8,)), dma((2,)), dma((2,)), dma((1,)), dma((1,)),
        ],
        compiler_params=pltpu.CompilerParams(
            collective_id=0, has_side_effects=True, vmem_limit_bytes=56 * 2**20
        ),
        name="jacobi",
    )(round_count, move_flag.T, row_weight.reshape(rows // B, B), col_scale.reshape(2, B), jacobian)


def solution(mesh):
    in_specs = (P("rows", "blk"), P("rows"), P("blk"), P(), P(None, "blk"))
    out_specs = (P("rows", "blk"), P("rows", "blk"))
    return jax.shard_map(
        per_device, mesh=mesh, in_specs=in_specs, out_specs=out_specs, check_vma=False
    )
```

```python
import functools

import jax
import jax.numpy as jnp
from jax import lax
from jax.experimental import pallas as pl
from jax.experimental.pallas import tpu as pltpu
from jax.sharding import PartitionSpec as P

MESH = pl.DeviceIdType.MESH
B = 128
ROUNDS = 24
CH = 256
N_Y = 4
ROUND = 3
AHEAD = 4
EARLY = 4
F32 = jnp.float32
BF16 = jnp.bfloat16


def split(x):
    high = x.astype(BF16)
    return high, (x - high.astype(F32)).astype(BF16)


def split_rest(x):
    high = x.astype(BF16)
    return high, x - high.astype(F32)


def rotation(first, second, cross, live):
    diff = second - first
    inverse = lax.rsqrt(diff * diff + 4.0 * cross * cross)
    square = 0.5 + 0.5 * (jnp.abs(diff) * inverse)
    scale = lax.rsqrt(square)
    sine = jnp.where(diff >= 0.0, cross, -cross) * inverse * scale
    return jnp.where(live, square * scale, 1.0), jnp.where(live, sine, 0.0)


def tile(k):
    return pl.ds(8 * k, 8)


def spaced(k, start=0):
    return pl.ds(start + k, 8, stride=16)


def inner_rounds(count, cross, out, q, upper, lower, a, c, e, d, ccol, scol):
    count = jnp.full((8, B), count, jnp.int32)
    lane = lax.broadcasted_iota(jnp.int32, (8, B), 1)
    sub = lax.broadcasted_iota(jnp.int32, (8, B), 0)

    def band(distance):
        row = (lane + (B - distance)) % B
        return row % 16, (row // 16) == sub

    bands = [band(distance) for distance in range(3)]

    def left(x, distance=1):
        return pltpu.roll(x, B - distance, 1)

    def total(x, distance):
        x = jnp.where(bands[distance][1], x, 0.0)
        return jnp.broadcast_to(jnp.sum(x, axis=0, keepdims=True), (8, B))

    def pick(ref, distance):
        acc = jnp.zeros((8, B), F32)
        for k in range(16):
            acc = jnp.where(bands[distance][0] == k, ref[tile(k), :], acc)
        return left(total(acc, distance), distance) if distance else total(acc, 0)

    def spread(cs, sn, place):
        for k in range(16):
            own = bands[0][1] & (bands[0][0] == k)
            ccol[place, tile(k), :] = jnp.broadcast_to(jnp.sum(jnp.where(own, cs, 0.0), axis=1, keepdims=True), (8, B))
            scol[place, tile(k), :] = jnp.broadcast_to(jnp.sum(jnp.where(own, sn, 0.0), axis=1, keepdims=True), (8, B))

    ccol[0] = jnp.transpose(cross[...])
    for k in range(16):
        c[tile(k), :] = cross[spaced(k), :]
        e[tile(k), :] = ccol[0, spaced(k), :]
    wide_lane = lax.broadcasted_iota(jnp.int32, (8, 2 * B), 1)
    wide_row = 16 * lax.broadcasted_iota(jnp.int32, (8, 2 * B), 0)
    for k in range(16):
        upper[tile(k), :] = (wide_lane == wide_row + k).astype(F32)
        lower[tile(k), :] = (wide_lane == wide_row + (B + k)).astype(F32)
    diag_a, diag_d, diag_c = pick(a, 0), pick(d, 0), pick(c, 0)
    near = pick(a, 1), pick(c, 1), pick(e, 1), pick(d, 1)
    cs, sn = rotation(diag_a, diag_d, diag_c, 0 < count)
    spread(cs, sn, 0)

    def one(index, place, carry):
        cs, sn, diag_a, diag_d, diag_c, near_a, near_c, near_e, near_d = carry
        new_c = left(sn) * (cs * near_a - sn * near_e) + left(cs) * (cs * near_c - sn * near_d)
        new_a = cs * (cs * diag_a - sn * diag_c) - sn * (cs * diag_c - sn * diag_d)
        new_d = left(sn * (sn * diag_a + cs * diag_c) + cs * (sn * diag_c + cs * diag_d))
        new = rotation(new_a, new_d, new_c, index + 1 < count)
        spread(*new, 1 - place)
        acc_a = acc_c = acc_d = acc_e = jnp.zeros((8, B), F32)
        first = None
        for k in range(16):
            before = tile((k - 1) % 16)
            ck, sk = ccol[place, tile(k), :], scol[place, tile(k), :]
            ak, bk, ek, dk = a[tile(k), :], c[tile(k), :], e[tile(k), :], d[tile(k), :]
            cw, sw = jnp.concatenate([ck, ck], 1), jnp.concatenate([sk, sk], 1)
            qu, ql = upper[tile(k), :], lower[tile(k), :]
            upper[tile(k), :] = cw * qu - sw * ql
            q2 = sw * qu + cw * ql
            a1 = ck * ak - sk * ek
            e1 = sk * ak + ck * ek
            b1 = ck * bk - sk * dk
            d1 = sk * bk + ck * dk
            a2 = a1 * cs - b1 * sn
            b2 = a1 * sn + b1 * cs
            e2 = e1 * cs - d1 * sn
            d2 = e1 * sn + d1 * cs
            acc_a = jnp.where(bands[1][0] == k, a2, acc_a)
            acc_c = jnp.where(bands[2][0] == k, b2, acc_c)
            acc_e = jnp.where(bands[0][0] == k, e2, acc_e)
            acc_d = jnp.where(bands[1][0] == k, d2, acc_d)
            a[tile(k), :] = a2
            c[tile(k), :] = left(b2)
            d3 = left(d2)
            if k == 0:
                first = (e2, d3, q2)
            else:
                lower[before, :] = q2
                e[before, :] = e2
                d[before, :] = d3
        e[tile(15), :] = pltpu.roll(first[0], 7, 0)
        d[tile(15), :] = pltpu.roll(first[1], 7, 0)
        lower[tile(15), :] = pltpu.roll(first[2], 7, 0)
        near = (left(total(acc_a, 1)), left(total(acc_c, 2), 2), left(total(acc_e, 0)), left(total(acc_d, 1), 2))
        return (*new, new_a, new_d, new_c, *near)

    def two(index, carry):
        return one(2 * index + 1, 1, one(2 * index, 0, carry))

    lax.fori_loop(0, ROUNDS // 2, two, (cs, sn, diag_a, diag_d, diag_c, *near))
    extra = ROUNDS - count
    surplus = [(extra >> bit) % 2 == 1 for bit in range(5)]
    tiles = [lower[tile(k), :] for k in range(16)]
    for bit in range(5):
        tiles = undo_rows(tiles, bit, surplus[bit])
    for k in range(16):
        q[spaced(k), :] = tiles[k][:, :B]
        q[spaced(k, B), :] = tiles[k][:, B:]
    out[:B, B:], out[B:, B:] = jnp.transpose(q[:B, :]), jnp.transpose(q[B:, :])
    for k in range(16):
        q[spaced(k), :] = upper[tile(k), :B]
        q[spaced(k, B), :] = upper[tile(k), B:]
    out[:B, :B], out[B:, :B] = jnp.transpose(q[:B, :]), jnp.transpose(q[B:, :])
    return surplus


def undo_rows(tiles, bit, on):
    move = 1 << bit
    moved = []
    for k in range(16):
        value = tiles[(k - move) % 16]
        moved.append(value if k >= move else pltpu.roll(value, 1, 0))
    return [jnp.where(on[0:1, 0:1], new, old) for new, old in zip(moved, tiles)]


def undo_moves(d, surplus):
    tiles = [d[tile(k), :] for k in range(16)]
    for bit in range(5):
        move = 1 << bit
        moved = []
        for k in range(16):
            value = pltpu.roll(tiles[(k - move) % 16], move, 1)
            moved.append(value if k >= move else pltpu.roll(value, 1, 0))
        tiles = [jnp.where(surplus[bit], new, old) for new, old in zip(moved, tiles)]
    return tiles


def body(
    counts, flags, weights_hbm, scales_hbm, x_hbm, out_hbm, w_out,
    x_in, s_in, t_far, q_in0, q_in1, p0a, p0b, p0c, p1a, p1b, p1c,
    x_send, x_recv, f_send, f_recv, q_send, q_recv, far_sem,
    weights, scales, x, s, t, tin, sin, u, v, r1, r2, g, hh, hl, q, qn, qa, qb, qhi, qmid, qlo, ra, rc, re, rd, ccol, scol,
    half, piece, full, cross, cross_half, own_piece, far_piece, cross_full, d_out, d_in, w1, w1in, w2, w2in,
    small_sem, load_sem, store_sem, t_send, t_recv, s_send, s_recv, u_send, u_recv,
    r_send, r_recv, core_send, core_recv, z_send, z_recv, far_send, far_recv, w_send, w_recv, d_send, d_recv,
):
    q_in, q_parts = (q_in0, q_in1), ((p0a, p0b, p0c), (p1a, p1b, p1c))
    row, blk = lax.axis_index("rows"), lax.axis_index("blk")
    n_blk = lax.axis_size("blk")
    z, core = row // 2, row % 2
    chunks = x.shape[0] // CH
    mid = (AHEAD + chunks) // 2
    next_blk = (blk + 1) % n_blk
    last_blk = (blk + n_blk - 1) % n_blk
    fwd, bwd = (row, next_blk), (row, last_blk)
    twin = (row + 1 - 2 * core, blk)
    peers = [(((z + i) % 8) * 2 + core, blk) for i in range(1, 8)]
    far = [(((z + i) % 8) * 2 + core, next_blk) for i in range(8)]
    far_from = [(((z + i) % 8) * 2 + core, last_blk) for i in range(8)]
    column = blk // N_Y * N_Y
    below = (row, column + (blk + N_Y - 1) % N_Y)
    above = (row, column + (blk + 1) % N_Y)
    last_hop = (row, (column + (blk + 2) % N_Y + 1) % n_blk)
    last_hop_from = (row, last_blk // N_Y * N_Y + (last_blk + 2) % N_Y)
    owner = row == blk
    next_owner = row == last_blk
    third_owner = row == (blk + n_blk - 2) % n_blk

    def at(c):
        return pl.ds(pl.multiple_of(c * CH, CH), CH)

    def load(c):
        return pltpu.make_async_copy(x_hbm.at[at(c), :], x.at[at(c), :], load_sem.at[c])

    small_loads = [
        pltpu.make_async_copy(weights_hbm, weights, small_sem.at[0]),
        pltpu.make_async_copy(scales_hbm, scales, small_sem.at[1]),
    ]
    for copy in small_loads:
        copy.start()
    lax.fori_loop(0, chunks, lambda c, _: (load(c).start(), 0)[1], 0)

    barrier = pltpu.get_barrier_semaphore()
    for device in [twin, fwd, above, last_hop_from] + peers + far_from:
        pl.semaphore_signal(barrier, inc=1, device_id=device, device_id_type=MESH)

    pl.semaphore_wait(barrier, 19)

    def remote(src, dst, send, recv, device):
        return pltpu.make_async_remote_copy(
            src_ref=src, dst_ref=dst, send_sem=send, recv_sem=recv, device_id=device, device_id_type=MESH
        )

    dims = (((0,), (0,)), ((), ()))

    def gram():
        hh[...] = jnp.zeros_like(hh)
        hl[...] = jnp.zeros_like(hl)

        for copy in small_loads:
            copy.wait()
        ccol[0, 0 : weights.shape[0], :] = weights[...]
        ccol[0, weights.shape[0] :, :] = jnp.zeros((B - weights.shape[0], B), F32)
        scol[0] = jnp.transpose(ccol[0])
        lanes = lax.broadcasted_iota(jnp.int32, (B, B), 1)
        scale = jnp.concatenate([scales[0:1, :], scales[1:2, :]], 1)

        def add(ahead, c, acc):
            load(c).wait()
            parts = []
            for i in range(CH // B):
                column = jnp.where(lanes == c * (CH // B) + i, scol[0], 0.0)
                column = jnp.sum(column, axis=1, keepdims=True)
                rows = pl.ds(pl.multiple_of(c * CH + i * B, B), B)
                parts.append(x[rows, :] * column * scale)
                x[rows, :] = parts[-1]
            if ahead:
                x_copy(c).start()
            high, low = split(jnp.concatenate(parts, 0))
            both = lax.dot_general(high, jnp.concatenate([high, low], 1), dims, preferred_element_type=F32)
            small = low.astype(F32)
            hh[...] = hh[...] + both[:, : 2 * B]
            hl[...] = hl[...] + both[:, 2 * B :]
            return acc + jnp.sum((small * small).reshape(CH // 8, 8, 2 * B), axis=0)

        small = lax.fori_loop(0, EARLY, functools.partial(add, True), jnp.zeros((8, 2 * B), F32))
        small = lax.fori_loop(EARLY, chunks, functools.partial(add, False), small)
        small = jnp.sum(small, axis=0, keepdims=True)
        rows = lax.broadcasted_iota(jnp.int32, (B, B), 0)
        cols = lax.broadcasted_iota(jnp.int32, (B, B), 1)
        for place, (i, j) in enumerate(((0, 0), (0, 1), (1, 1))):
            here, there = pl.ds(i * B, B), pl.ds(j * B, B)
            block = hh[here, there] + (hl[here, there] + jnp.transpose(hl[there, here]))
            if i == j:
                block = block + jnp.where(rows == cols, small[:, i * B : (i + 1) * B], 0.0)
            g[pl.ds(place * B, B), :] = block

    def exchange(index, src, dst):
        copy = remote(src, dst, core_send.at[index], core_recv.at[index], twin)
        copy.start()
        copy.wait()

    def share_start(step, ref, own):
        copies = []
        for i, peer in enumerate(peers):
            copies.append(remote(
                ref.at[own, :], ref.at[own, :], z_send.at[step, 7 + i], z_recv.at[step, 7 + i], peer
            ))
            copies[-1].start()
        return copies

    def share(step, ref, own):
        for copy in share_start(step, ref, own):
            copy.wait()

    def reduce_all():
        mine = pl.ds(pl.multiple_of(core * 192, 8), 192)
        other = pl.ds(pl.multiple_of((1 - core) * 192, 8), 192)
        own = pl.ds(pl.multiple_of(core * 192 + z * 24, 8), 24)
        exchange(0, g.at[other, :], half.at[:, :])
        g[mine, :] = g[mine, :] + half[...]
        copies = []
        for i, peer in enumerate(peers):
            rows = pl.ds(pl.multiple_of(core * 192 + (peer[0] // 2) * 24, 8), 24)
            copies.append(remote(g.at[rows, :], piece.at[i], z_send.at[0, i], z_recv.at[0, i], peer))
            copies[-1].start()
        for copy in copies:
            copy.wait()
        total = g[own, :]
        for i in range(7):
            total = total + piece[i]
        full[own, :] = total
        share(0, full, own)
        exchange(1, full.at[mine, :], full.at[mine, :])

    def reduce_cross(started):
        mine = pl.ds(pl.multiple_of(core * 64, 8), 64)
        other = pl.ds(pl.multiple_of((1 - core) * 64, 8), 64)
        own = pl.ds(pl.multiple_of(core * 64 + z * 8, 8), 8)
        exchange(2, cross.at[:, other, :], cross_half)
        cross[:, mine, :] = cross[:, mine, :] + cross_half[...]
        copies = []
        for i, device in enumerate(far):
            rows = pl.ds(pl.multiple_of(core * 64 + (device[0] // 2) * 8, 8), 8)
            copies.append(remote(cross.at[1, rows, :], far_piece.at[i], far_send.at[i], far_recv.at[i], device))
            copies[-1].start()
        for i, peer in enumerate(peers):
            rows = pl.ds(pl.multiple_of(core * 64 + (peer[0] // 2) * 8, 8), 8)
            copies.append(remote(cross.at[0, rows, :], own_piece.at[i], z_send.at[1, i], z_recv.at[1, i], peer))
            copies[-1].start()
        started()
        for copy in copies:
            copy.wait()
        total = cross[0, own, :] + far_piece[0]
        for i in range(7):
            total = total + (own_piece[i] + far_piece[i + 1])
        cross_full[own, :] = total
        share(1, cross_full, own)
        exchange(3, cross_full.at[mine, :], cross_full.at[mine, :])

    def arrange(step):
        left = jnp.full((8, B), flags[0, step], jnp.int32) == 1
        for k in range(32):
            qa, qb = q[tile(k), 0:B], q[tile(k), B : 2 * B]
            q[tile(k), 0:B] = jnp.where(left, qb, qa)
            q[tile(k), B : 2 * B] = jnp.where(left, qa, qb)
        three(q, qhi, qmid, qlo)
        return left

    def three(source, high, middle, low):
        high[...], rest = split_rest(source[...])
        middle[...], rest = split_rest(rest)
        low[...] = rest.astype(BF16)

    def q_copy(step):
        own = pl.ds(pl.multiple_of(core * B + z * 16, 16), 16)
        source = q.at[own, :] if step == 0 else q.at[own, B : 2 * B]
        return remote(source, q_in[step].at[own, :], q_send.at[step], q_recv.at[step], fwd)

    def gather_begin(step):
        own = pl.ds(pl.multiple_of(core * B + z * 16, 16), 16)
        q_copy(step).wait()
        return share_start(2 + step, q_in[step], own)

    def gather_middle(step, copies):
        mine = pl.ds(pl.multiple_of(core * B, B), B)
        for copy in copies:
            copy.wait()
        last = remote(
            q_in[step].at[mine, :], q_in[step].at[mine, :], core_send.at[4 + step], core_recv.at[4 + step], twin
        )
        last.start()
        return last

    def gather_end(step, last):
        last.wait()
        three(q_in[step], *q_parts[step])

    def x_copy(c):
        return remote(x.at[at(c), :], x_in.at[at(c), :], x_send.at[c], x_recv.at[c], fwd)

    def far_copy(c):
        return remote(tin.at[at(c), :], t_far.at[at(c), :], f_send.at[c], f_recv.at[c], fwd)

    def multiply(block, parts=(qhi, qmid, qlo)):
        high, low = split(block)
        qh = parts[0][...]
        out = jnp.dot(high, parts[2][...], preferred_element_type=F32)
        out = out + jnp.dot(low, qh, preferred_element_type=F32)
        out = out + jnp.dot(high, parts[1][...], preferred_element_type=F32)
        return out + jnp.dot(high, qh, preferred_element_type=F32)

    def t_copy(c):
        return remote(t.at[at(c), :], tin.at[at(c), :], t_send.at[c], t_recv.at[c], fwd)

    def s_copy(c):
        return remote(s.at[at(c), :], sin.at[at(c - mid), :], s_send.at[c - mid], s_recv.at[c - mid], bwd)

    def u_copy(c):
        return remote(u.at[at(c), :], out_hbm.at[at(c), B : 2 * B], u_send.at[c], u_recv.at[c], fwd)

    def relay(hop, c):
        i = c - AHEAD
        if hop == 0:
            return remote(u.at[at(c), :], r1.at[at(i), :], r_send.at[0, i], r_recv.at[0, i], below)
        if hop == 1:
            return remote(r1.at[at(i), :], r2.at[at(i), :], r_send.at[1, i], r_recv.at[1, i], below)
        return remote(r2.at[at(i), :], out_hbm.at[at(c), B : 2 * B], r_send.at[2, i], u_recv.at[c], last_hop)

    def w_copy(step):
        if step == 0:
            return remote(w1.at[:, B : 2 * B], w1in, w_send.at[0], w_recv.at[0], fwd)
        return remote(w2.at[:, B : 2 * B], w2in, w_send.at[1], w_recv.at[1], fwd)

    d_copy = remote(d_out, d_in, d_send.at[0], d_recv.at[0], fwd)

    gram()
    reduce_all()
    lax.fori_loop(EARLY, AHEAD, lambda c, _: (x_copy(c).start(), 0)[1], 0)
    for k in range(16):
        ra[tile(k), :] = full[spaced(k), :]
        rd[tile(k), :] = full[spaced(k, 2 * B), :]
    surplus = inner_rounds(counts[0], full.at[pl.ds(B, B), :], q, qn, qa, qb, ra, rc, re, rd, ccol, scol)
    left = arrange(0)

    def rotate(c):
        y = multiply(x[at(c), :])
        s[at(c), :] = y[:, :B]
        t[at(c), :] = y[:, B:]

    def first_step(i, _):
        rotate(AHEAD + i)
        t_copy(AHEAD + i).start()
        rotate(mid + i)
        s_copy(mid + i).start()
        return 0

    q_copy(0).start()
    lax.fori_loop(0, mid - AHEAD, first_step, 0)

    def rotate_own(c, _):
        s[at(c), :] = multiply(x[at(c), :])[:, :B]
        return 0

    lax.fori_loop(0, AHEAD, rotate_own, 0)

    for k, second in enumerate(undo_moves(rd, surplus)):
        first = ra[tile(k), :]
        ra[tile(k), :] = jnp.where(left, second, first)
        d_out[tile(k), :] = jnp.where(left, first, second)
    d_copy.start()

    @pl.when(owner)
    def _():
        w1[...] = q[...]
        w_copy(0).start()

    @pl.when(jnp.logical_not(owner))
    def _():
        w1[...] = jnp.zeros_like(w1)

    @pl.when(jnp.logical_not(next_owner))
    def _():
        w1in[...] = jnp.zeros_like(w1in)

    hh[...] = jnp.zeros_like(hh)
    hl[...] = jnp.zeros_like(hl)

    def inner(one, two):
        one, two = jnp.concatenate(split(one), 1), jnp.concatenate(split(two), 1)
        return lax.dot_general(one, two, dims, preferred_element_type=F32)

    pending = gather_begin(0)

    def meet_own(c, _):
        x_copy(c).wait_recv()
        y = multiply(x_in[at(c), :], q_parts[0])
        s_in[at(c), :] = y[:, :B]
        tin[at(c), :] = y[:, B:]
        hh[...] = hh[...] + inner(s[at(c), :], y[:, B:])
        return 0

    def meet(i, _):
        c = AHEAD + i
        t_copy(c).wait_recv()
        hh[...] = hh[...] + inner(s[at(c), :], tin[at(c), :])
        s_copy(mid + i).wait_recv()
        hl[...] = hl[...] + inner(sin[at(i), :], t[at(mid + i), :])
        return 0

    pairs = mid - AHEAD
    lax.fori_loop(0, pairs // 3, meet, 0)
    pending = gather_middle(0, pending)
    lax.fori_loop(pairs // 3, pairs * 2 // 3, meet, 0)
    gather_end(0, pending)
    lax.fori_loop(0, AHEAD, meet_own, 0)
    lax.fori_loop(pairs * 2 // 3, pairs, meet, 0)
    for place, ref in enumerate((hh, hl)):
        mixed = ref[:B, B:] + ref[B:, :B]
        cross[place] = ref[:B, :B] + (mixed + ref[B:, B:])

    def send_rest():
        lax.fori_loop(mid, chunks, lambda c, _: (t_copy(c).start(), 0)[1], 0)
        lax.fori_loop(0, AHEAD, lambda c, _: (far_copy(c).start(), 0)[1], 0)

    reduce_cross(send_rest)
    d_copy.wait()
    for k in range(16):
        rd[tile(k), :] = d_in[tile(k), :]
    inner_rounds(counts[1], cross_full, q, qn, qa, qb, ra, rc, re, rd, ccol, scol)
    arrange(1)
    q_copy(1).start()

    def stay_copy(c):
        return pltpu.make_async_copy(v.at[at(c), :], out_hbm.at[at(c), 0:B], store_sem.at[c])

    def second_step(c, send):
        y = multiply(jnp.concatenate([s[at(c), :], tin[at(c), :]], 1))
        u[at(c), :] = y[:, B:]
        send(c).start()
        v[at(c), :] = y[:, :B]
        stay_copy(c).start()

    def round_step(c, _):
        second_step(c, functools.partial(relay, 0))
        return 0

    def near_step(c, _):
        second_step(c, u_copy)
        return 0

    def late_step(c, _):
        t_copy(c).wait_recv()
        second_step(c, u_copy)
        return 0

    def own_step(c, _):
        y = multiply(jnp.concatenate([s[at(c), :], tin[at(c), :]], 1))
        v[at(c), :] = y[:, :B]
        stay_copy(c).start()
        return 0

    def far_store(c):
        return pltpu.make_async_copy(u.at[at(c), :], out_hbm.at[at(c), B : 2 * B], far_sem.at[c])

    def far_step(c, _):
        far_copy(c).wait_recv()
        u[at(c), :] = multiply(jnp.concatenate([s_in[at(c), :], t_far[at(c), :]], 1), q_parts[1])
        far_store(c).start()
        return 0

    lax.fori_loop(AHEAD, AHEAD + ROUND, round_step, 0)
    lax.fori_loop(AHEAD + ROUND, mid, near_step, 0)
    lax.fori_loop(mid, chunks, late_step, 0)
    lax.fori_loop(0, AHEAD, own_step, 0)
    pending = gather_begin(1)

    @pl.when(next_owner)
    def _():
        w_copy(0).wait_recv()

    w2[...] = multiply(jnp.concatenate([w1[:, :B], w1in[...]], 1))
    w_out[:, :B] = w2[:, :B]

    @pl.when(jnp.logical_or(owner, next_owner))
    def _():
        w_copy(1).start()

    @pl.when(jnp.logical_not(jnp.logical_or(next_owner, third_owner)))
    def _():
        w_out[:, B:] = jnp.zeros((2 * B, B), F32)

    for hop in (0, 1):

        def pass_on(c, _, hop=hop):
            relay(hop, c).wait_recv()
            relay(hop + 1, c).start()
            return 0

        lax.fori_loop(AHEAD, AHEAD + ROUND, pass_on, 0)
        if hop == 0:
            pending = gather_middle(1, pending)

    gather_end(1, pending)
    lax.fori_loop(0, AHEAD, far_step, 0)

    def finish_round(c, _):
        for hop in range(3):
            relay(hop, c).wait_send()
        return 0

    lax.fori_loop(AHEAD, AHEAD + ROUND, finish_round, 0)
    lax.fori_loop(AHEAD + ROUND, chunks, lambda c, _: (u_copy(c).wait_send(), 0)[1], 0)

    def finish(c, _):
        t_copy(c).wait_send()
        u_copy(c).wait_recv()
        stay_copy(c).wait()
        return 0

    def finish_own(c, _):
        x_copy(c).wait_send()
        far_copy(c).wait_send()
        far_store(c).wait()
        stay_copy(c).wait()
        return 0

    lax.fori_loop(AHEAD, chunks, finish, 0)
    lax.fori_loop(0, AHEAD, finish_own, 0)
    lax.fori_loop(mid, chunks, lambda c, _: (s_copy(c).wait_send(), 0)[1], 0)

    @pl.when(owner)
    def _():
        w_copy(0).wait_send()

    @pl.when(jnp.logical_or(owner, next_owner))
    def _():
        w_copy(1).wait_send()

    @pl.when(jnp.logical_or(next_owner, third_owner))
    def _():
        w_copy(1).wait_recv()
        w_out[:, B:] = w2in[...]


def per_device(jacobian, row_weight, col_scale, round_count, move_flag):
    rows = jacobian.shape[0]
    chunks = rows // CH
    anywhere = pl.BlockSpec(memory_space=pl.ANY)
    vmem = pl.BlockSpec(memory_space=pltpu.VMEM)
    hbm = pl.BlockSpec(memory_space=pltpu.HBM)
    smem = pl.BlockSpec(memory_space=pltpu.SMEM)
    dma = pltpu.SemaphoreType.DMA
    square = pltpu.VMEM((B, B), F32)
    double = pltpu.VMEM((2, B, B), F32)
    wide = pltpu.VMEM((2 * B, 2 * B), F32)
    narrow = pltpu.VMEM((2 * B, 2 * B), BF16)
    tall = pltpu.VMEM((2 * B, B), F32)
    flat = pltpu.VMEM((B, 2 * B), F32)
    column = pltpu.VMEM((rows, B), F32)
    ahead = pltpu.VMEM((AHEAD * CH, B), F32)
    thin = pltpu.VMEM((2 * B, B), BF16)
    relayed = pltpu.VMEM((ROUND * CH, B), F32)
    return pl.pallas_call(
        body,
        out_shape=(
            jax.ShapeDtypeStruct((rows, 2 * B), F32),
            jax.ShapeDtypeStruct((2 * B, 2 * B), F32),
        ),
        in_specs=[smem, smem, hbm, hbm, hbm],
        out_specs=(anywhere, vmem),
        scratch_shapes=[
            pltpu.VMEM((AHEAD * CH, 2 * B), F32), ahead, ahead, wide, tall,
            narrow, narrow, narrow, thin, thin, thin,
            dma((AHEAD,)), dma((AHEAD,)), dma((AHEAD,)), dma((AHEAD,)), dma((2,)), dma((2,)), dma((AHEAD,)),
            pltpu.VMEM((rows // B, B), F32), pltpu.VMEM((2, B), F32),
            pltpu.VMEM((rows, 2 * B), F32), column, column, column, pltpu.VMEM((rows // 2, B), F32), column, column,
            relayed, relayed,
            pltpu.VMEM((3 * B, B), F32), wide, wide, wide, tall, flat, flat, narrow, narrow, narrow,
            square, square, square, square, double, double,
            pltpu.VMEM((192, B), F32), pltpu.VMEM((7, 24, B), F32), pltpu.VMEM((3 * B, B), F32),
            pltpu.VMEM((2, B, B), F32), pltpu.VMEM((2, 64, B), F32),
            pltpu.VMEM((7, 8, B), F32), pltpu.VMEM((8, 8, B), F32), square, square, square,
            wide, tall, wide, tall,
            dma((2,)), dma((chunks,)), dma((chunks,)), dma((chunks,)), dma((chunks,)),
            dma((chunks // 2,)), dma((chunks // 2,)), dma((chunks,)), dma((chunks,)),
            dma((3, ROUND)), dma((2, ROUND)), dma((6,)), dma((6,)), dma((4, 14)), dma((4, 14)), dma((8,)), dma((8,)), dma((2,)), dma((2,)), dma((1,)), dma((1,)),
        ],
        compiler_params=pltpu.CompilerParams(
            collective_id=0, has_side_effects=True, vmem_limit_bytes=46 * 2**20
        ),
        name="jacobi",
    )(round_count, move_flag.T, row_weight.reshape(rows // B, B), col_scale.reshape(2, B), jacobian)


def solution(mesh):
    in_specs = (P("rows", "blk"), P("rows"), P("blk"), P(), P(None, "blk"))
    out_specs = (P("rows", "blk"), P("rows", "blk"))
    return jax.shard_map(
        per_device, mesh=mesh, in_specs=in_specs, out_specs=out_specs, check_vma=False
    )
```
